32 devices in a mesh: gx: 4 (over y, x), gy: 2 (over core), gz: 4 (over z).
Axes of the slice: x: 2, y: 2, z: 4, core: 2. Of those that a mesh axis runs over, the one named last changes fastest.
Arguments:
- velocity: float32 [3, 32, 16, 512], P(None, 'gx', 'gy', 'gz'), may hold values from -6 to 6
- features: bfloat16 [16, 32, 16, 512], P(None, 'gx', 'gy', 'gz'), may hold values from -6 to 6
- density: float32 [32, 16, 512], P('gx', 'gy', 'gz'), may hold values from 0.5 to 2
- target: float32 [3, 32, 16, 512], P(None, 'gx', 'gy', 'gz'), may hold values from -6 to 6
- weight_in: bfloat16 [16, 64], replicated, may hold values from -1.5 to 1.5
- bias_in: float32 [64], replicated, may hold values from -3 to 3
- weight_out: bfloat16 [64, 3], replicated, may hold values from -0.75 to 0.75
- open_faces: int32 [6], replicated, may hold values from 0 to 1
Outputs:
- new_velocity: float32 [3, 32, 16, 512], P(None, 'gx', 'gy', 'gz')
- grad_weight_in: float32 [16, 64], replicated
- grad_bias_in: float32 [64], replicated
- grad_weight_out: float32 [64, 3], replicated
The draws below stay inside these ranges and needn't reach their ends.
Inputs may be any that keep to these rules, and one draw needn't show every extreme that they name: `open_faces`: entries in the order low first, high first, low second, high second, low third, high third face; 1 marks an open face (pressure zero beyond it), 0 a wall.
All inputs are finite; a program needn't handle non-finite values.
Results may differ from the reference program's by a relative error of at most 0.0012.
Values sent between devices are 32-bit elements; how exact they have to be, the bound alone decides.
A program may use at most 128 MiB of HBM per device.

```python
import math
import jax
import jax.numpy as jnp
from jax import lax

FEAT = 16
HIDDEN_SIZE = 64
CYCLES = 2
SWEEPS = 3
COARSE_SWEEPS = 6
NX = 32
NY = 16
NZ = 512


PERIOD_MAIN = 40.0


PERIOD_SIDE = 56.0


def smooth_flux(key):
    phase_key, amplitude_key, rough_key = jax.random.split(key, 3)
    phases = jax.random.uniform(phase_key, (3, 2), jnp.float32, 0.0, 2.0 * math.pi)
    amplitude = 3.0 * jax.random.uniform(amplitude_key, (3,), jnp.float32, 0.6, 1.0)
    rough_part = jnp.clip(jax.random.normal(rough_key, (3, NX, NY, NZ), jnp.float32), -2.5, 2.5)
    positions = (jnp.arange(NX, dtype=jnp.float32).reshape(-1, 1, 1), jnp.arange(NY, dtype=jnp.float32).reshape(1, -1, 1), jnp.arange(NZ, dtype=jnp.float32).reshape(1, 1, -1))
    components = []
    for direction in range(3):
        lengthwise = jnp.sin(2.0 * math.pi * positions[direction] / PERIOD_MAIN + phases[direction, 0])
        crosswise = 0.75 + 0.25 * jnp.cos(2.0 * math.pi * positions[(direction + 1) % 3] / PERIOD_SIDE + phases[direction, 1])
        components.append(jnp.broadcast_to(amplitude[direction] * lengthwise * crosswise, (NX, NY, NZ)))
    return jnp.stack(components) + rough_part


def draw_velocity(key, part):
    return smooth_flux(jax.random.fold_in(key, 11))


def draw_target(key, part):
    return smooth_flux(jax.random.fold_in(key, 23))


def touch_ends(array, stream_key, least, high):
    longest = array.shape.index(max(array.shape))
    spots = []
    for shift in (0, 1):
        where = [jax.random.randint(jax.random.fold_in(stream_key, axis), (), 0, length) for axis, length in enumerate(array.shape)]
        where[longest] = (where[longest] + shift) % array.shape[longest]
        spots.append(tuple(where))
    return array.at[spots[0]].set(least).at[spots[1]].set(high)


def block_scale(rng, shape, cuts, low, largest):
    gain = 1.0
    for dim, shards_of in cuts:
        draws = jax.random.uniform(jax.random.fold_in(jax.random.fold_in(rng, 6), dim), (shards_of,), jnp.float32, low / len(cuts), largest / len(cuts))
        gain = gain * jnp.repeat(jnp.exp(draws), shape[dim] // shards_of).reshape((-1,) + (1,) * (len(shape) - 1 - dim))
    return gain


def gaussian(stream_key, extent, deviation, most, pieces=(), kind=jnp.bfloat16):
    gain = block_scale(stream_key, extent, pieces, -0.22, 0.18) if pieces else 1.0
    array = jax.random.normal(stream_key, extent, jnp.float32) * deviation * gain
    return jnp.minimum(jnp.maximum(array, -most), most).astype(kind)


def setup_inputs(seed: int = 0) -> dict:
    key_of = jax.random.split(jax.random.key(seed), 9)
    return {
        "velocity": draw_velocity(jax.random.fold_in(key_of[8], 71), 0),
        "features": gaussian(key_of[1], (FEAT, NX, NY, NZ), 1.0, 6.0, ((1, 4), (2, 2), (3, 4))),
        "density": jnp.clip(jnp.exp(math.log(2.0) - 1.3862944 * jax.random.uniform(key_of[2], (NX, NY, NZ), jnp.float32) ** block_scale(key_of[2], (NX, NY, NZ), ((0, 4), (1, 2), (2, 4)), -0.2, 0.2)), 0.5, 2.0),
        "target": draw_target(jax.random.fold_in(key_of[8], 71), 0),
        "weight_in": gaussian(key_of[4], (FEAT, HIDDEN_SIZE), FEAT ** -0.5, 1.5),
        "bias_in": gaussian(key_of[5], (HIDDEN_SIZE,), 0.5, 3.0, (), jnp.float32),
        "weight_out": gaussian(key_of[6], (HIDDEN_SIZE, 3), HIDDEN_SIZE ** -0.5, 0.75),
        "open_faces": touch_ends(jax.random.randint(key_of[7], (6,), 0, 2), jax.random.fold_in(key_of[7], 1), 0, 1).astype(jnp.int32),
    }


RELAXATION = 0.8
MASS_SHIFT = 0.05
SHAPES = ((-1, 1, 1), (1, -1, 1), (1, 1, -1))


def zero_padded(field):
    return jnp.pad(field, 1)


def edge_factors(length, offset, whole_length, lower_flag, upper_flag):
    position = jnp.arange(length, dtype=jnp.int32) + offset
    lower = jnp.where(position == 0, lower_flag.astype(jnp.float32), jnp.float32(1.0))
    upper = jnp.where(position == whole_length - 1, upper_flag.astype(jnp.float32), jnp.float32(1.0))
    return lower, upper


def coefficients(padded_density, factors, weight):
    centre = padded_density[1:-1, 1:-1, 1:-1]
    following = (padded_density[2:, 1:-1, 1:-1], padded_density[1:-1, 2:, 1:-1], padded_density[1:-1, 1:-1, 2:])
    preceding = (padded_density[:-2, 1:-1, 1:-1], padded_density[1:-1, :-2, 1:-1], padded_density[1:-1, 1:-1, :-2])
    upper_coefs = tuple(weight * 2.0 / (centre + following[direction]) * factors[direction][1].reshape(SHAPES[direction]) for direction in range(3))
    lower_coefs = tuple(weight * 2.0 / (centre + preceding[direction]) * factors[direction][0].reshape(SHAPES[direction]) for direction in range(3))
    diagonal = MASS_SHIFT + upper_coefs[0] + lower_coefs[0] + upper_coefs[1] + lower_coefs[1] + upper_coefs[2] + lower_coefs[2]
    return upper_coefs, lower_coefs, diagonal


def neighbour_sum(padded_field, upper_coefs, lower_coefs):
    summed = upper_coefs[0] * padded_field[2:, 1:-1, 1:-1] + lower_coefs[0] * padded_field[:-2, 1:-1, 1:-1]
    summed = summed + upper_coefs[1] * padded_field[1:-1, 2:, 1:-1] + lower_coefs[1] * padded_field[1:-1, :-2, 1:-1]
    summed = summed + upper_coefs[2] * padded_field[1:-1, 1:-1, 2:] + lower_coefs[2] * padded_field[1:-1, 1:-1, :-2]
    return summed


def apply_level(field, level_data):
    return level_data[3] * field - neighbour_sum(level_data[0](field), level_data[1], level_data[2])


def smooth_once(iterate, source, level_data):
    return iterate + RELAXATION * (source - apply_level(iterate, level_data)) / level_data[3]


def relax_from_zero(source, level_data, sweeps_count):
    iterate = RELAXATION * source / level_data[3]
    for repeat in range(sweeps_count - 1):
        iterate = smooth_once(iterate, source, level_data)
    return iterate


def restrict(field):
    span_first, span_second, span_third = field.shape
    return field.reshape(span_first // 2, 2, span_second // 2, 2, span_third // 2, 2).mean(axis=(1, 3, 5))


def prolong(field):
    span_first, span_second, span_third = field.shape
    spread = jnp.broadcast_to(field[:, None, :, None, :, None], (span_first, 2, span_second, 2, span_third, 2))
    return spread.reshape(2 * span_first, 2 * span_second, 2 * span_third)


def multigrid_cycle(source, levels, coarse_solve):
    level_data = levels[0]
    iterate = relax_from_zero(source, level_data, SWEEPS)
    residue = source - apply_level(iterate, level_data)
    if len(levels) > 1:
        correction = multigrid_cycle(restrict(residue), levels[1:], coarse_solve)
    else:
        correction = coarse_solve(restrict(residue))
    iterate = iterate + prolong(correction)
    for repeat in range(SWEEPS):
        iterate = smooth_once(iterate, source, level_data)
    return iterate


def pressure_solve(source, levels, coarse_solve):
    iterate = multigrid_cycle(source, levels, coarse_solve)
    for repeat in range(CYCLES - 1):
        iterate = iterate + multigrid_cycle(source - apply_level(iterate, levels[0]), levels, coarse_solve)
    return iterate


def divergence(fluxes, padder):
    first = padder(fluxes[0])[:-2, 1:-1, 1:-1]
    second = padder(fluxes[1])[1:-1, :-2, 1:-1]
    third = padder(fluxes[2])[1:-1, 1:-1, :-2]
    return (fluxes[0] - first) + (fluxes[1] - second) + (fluxes[2] - third)


def upward_differences(field, padder):
    padded = padder(field)
    return (padded[2:, 1:-1, 1:-1] - field, padded[1:-1, 2:, 1:-1] - field, padded[1:-1, 1:-1, 2:] - field)


def closure_plane(feature_plane, weight_in, bias_in, weight_out):
    columns = feature_plane.reshape(feature_plane.shape[0], -1)
    before = jnp.dot(weight_in.T, columns, preferred_element_type=jnp.float32) + bias_in[:, None]
    gate = jax.nn.sigmoid(before)
    hidden = (before * gate).astype(jnp.bfloat16)
    output = jnp.dot(weight_out.T, hidden, preferred_element_type=jnp.float32)
    return output.reshape((3,) + feature_plane.shape[1:])


def closure_field(features, weight_in, bias_in, weight_out):
    def one_plane(index):
        feature_plane = lax.dynamic_index_in_dim(features, index, 1, keepdims=False)
        return closure_plane(feature_plane, weight_in, bias_in, weight_out)

    stacked = lax.map(one_plane, jnp.arange(features.shape[1], dtype=jnp.int32))
    return jnp.moveaxis(stacked, 0, 1)


def gradient_plane(totals, feature_plane, grad_plane, weight_in, bias_in, weight_out):
    columns = feature_plane.reshape(feature_plane.shape[0], -1)
    before = jnp.dot(weight_in.T, columns, preferred_element_type=jnp.float32) + bias_in[:, None]
    gate = jax.nn.sigmoid(before)
    hidden = (before * gate).astype(jnp.bfloat16)
    upstream = grad_plane.reshape(3, -1).astype(jnp.bfloat16)
    grad_out = lax.dot_general(hidden, upstream, (((1,), (1,)), ((), ())), preferred_element_type=jnp.float32)
    grad_hidden = jnp.dot(weight_out, upstream, preferred_element_type=jnp.float32)
    grad_before = grad_hidden * (gate * (1.0 + before * (1.0 - gate)))
    grad_bias = jnp.sum(grad_before, axis=1)
    grad_in = lax.dot_general(columns, grad_before.astype(jnp.bfloat16), (((1,), (1,)), ((), ())), preferred_element_type=jnp.float32)
    return (totals[0] + grad_in, totals[1] + grad_bias, totals[2] + grad_out)


def closure_gradients(features, grad_correction, weight_in, bias_in, weight_out):
    def step_plane(totals, index):
        feature_plane = lax.dynamic_index_in_dim(features, index, 1, keepdims=False)
        grad_plane = lax.dynamic_index_in_dim(grad_correction, index, 1, keepdims=False)
        return gradient_plane(totals, feature_plane, grad_plane, weight_in, bias_in, weight_out), None

    start = (jnp.zeros(weight_in.shape, jnp.float32), jnp.zeros(bias_in.shape, jnp.float32), jnp.zeros(weight_out.shape, jnp.float32))
    totals, unused = lax.scan(step_plane, start, jnp.arange(features.shape[1], dtype=jnp.int32))
    return totals


def training_step(velocity, features, target, weight_in, bias_in, weight_out, levels, coarse_solve, fine_factors, cells_total):
    padder = levels[0][0]
    upper_coefs = levels[0][1]
    outlets = tuple(fine_factors[direction][1].reshape(SHAPES[direction]) for direction in range(3))
    correction = closure_field(features, weight_in, bias_in, weight_out)
    fluxes = tuple((velocity[direction] + correction[direction]) * outlets[direction] for direction in range(3))
    source = -divergence(fluxes, padder)
    pressure = pressure_solve(source, levels, coarse_solve)
    rises = upward_differences(pressure, padder)
    new_velocity = jnp.stack([fluxes[direction] - upper_coefs[direction] * rises[direction] for direction in range(3)])
    misfit = (new_velocity - target) / cells_total
    weighted = tuple(upper_coefs[direction] * misfit[direction] for direction in range(3))
    grad_pressure = divergence(weighted, padder)
    grad_source = pressure_solve(grad_pressure, levels, coarse_solve)
    drops = upward_differences(grad_source, padder)
    grad_correction = jnp.stack([(misfit[direction] + drops[direction]) * outlets[direction] for direction in range(3)])
    totals = closure_gradients(features, grad_correction, weight_in, bias_in, weight_out)
    return new_velocity, totals


def reference(velocity, features, density, target, weight_in, bias_in, weight_out, open_faces):
    def level_factors(shape_now):
        return tuple(edge_factors(shape_now[direction], 0, shape_now[direction], open_faces[2 * direction], open_faces[2 * direction + 1]) for direction in range(3))

    def make_level(level_density, weight):
        upper_coefs, lower_coefs, diagonal = coefficients(zero_padded(level_density), level_factors(level_density.shape), weight)
        return (zero_padded, upper_coefs, lower_coefs, diagonal)

    density_one = restrict(density)
    density_two = restrict(density_one)
    levels = (make_level(density, 1.0), make_level(density_one, 0.25))
    coarse_level = make_level(density_two, 0.0625)

    def coarse_solve(source):
        return relax_from_zero(source, coarse_level, COARSE_SWEEPS)

    new_velocity, totals = training_step(velocity, features, target, weight_in, bias_in, weight_out, levels, coarse_solve, level_factors(density.shape), density.size)
    return (new_velocity, totals[0], totals[1], totals[2])
```

```python
import functools

import jax
import jax.numpy as jnp
from jax import lax
from jax.experimental import pallas as pl
from jax.experimental.pallas import tpu as pltpu
from jax.sharding import PartitionSpec as P

SWEEPS = 3
COARSE_SWEEPS = 6


RELAXATION = 0.8
MASS_SHIFT = 0.05
SHAPES = ((-1, 1, 1), (1, -1, 1), (1, 1, -1))


def with_halo(shard, sides, width):
    for axis, dim in sides:
        count, length = (lax.axis_size(axis), shard.shape[dim])
        up = [(i, (i + 1) % count) for i in range(count - 1)]
        down = [(j, i) for i, j in up]
        last = lax.slice_in_dim(shard, length - width, length, axis=dim)
        leading = lax.slice_in_dim(shard, 0, width, axis=dim)
        before = lax.ppermute(last, axis, up)
        after = lax.ppermute(leading, axis, down)
        shard = jnp.concatenate([before, shard, after], axis=dim)
    return shard


def zero_padded(field):
    return jnp.pad(field, 1)


def halo_padded(field):
    return with_halo(field, (("gx", 0), ("gy", 1), ("gz", 2)), 1)


def deep_padded(field):
    return with_halo(field, (("gx", 0), ("gy", 1), ("gz", 2)), SWEEPS)


def deep_coefs(level_data):
    stacked = jnp.stack(list(level_data[1]) + list(level_data[2]) + [level_data[3]])
    extended = with_halo(stacked, (("gx", 1), ("gy", 2), ("gz", 3)), SWEEPS)
    diagonal = extended[6]
    safe_diagonal = jnp.where(diagonal > 0.0, diagonal, jnp.float32(1.0))
    return (
        (extended[0], extended[1], extended[2]),
        (extended[3], extended[4], extended[5]),
        diagonal,
        safe_diagonal,
    )


def trimmed(field, margin):
    span_first, span_second, span_third = field.shape
    return field[
        margin : span_first - margin, margin : span_second - margin, margin : span_third - margin
    ]


def apply_inner(iterate, extended, width):
    margin = SWEEPS - (width - 1)
    uppers = tuple((trimmed(extended[0][direction], margin) for direction in range(3)))
    lowers = tuple((trimmed(extended[1][direction], margin) for direction in range(3)))
    diagonal = trimmed(extended[2], margin)
    summed = neighbour_sum(iterate, uppers, lowers)
    return diagonal * iterate[1:-1, 1:-1, 1:-1] - summed


def sweep_inner(iterate, source_ext, extended, width):
    margin = SWEEPS - (width - 1)
    residue = trimmed(source_ext, margin) - apply_inner(iterate, extended, width)
    return iterate[1:-1, 1:-1, 1:-1] + RELAXATION * residue / trimmed(extended[3], margin)


def gather_whole(coarse_piece):
    span_first, span_second, span_third = coarse_piece.shape
    flattened = coarse_piece.reshape(1, span_first * span_second * span_third)
    gathered = lax.all_gather(flattened, ("gx", "gy", "gz"), axis=0, tiled=True)
    blocks = gathered.reshape(
        lax.axis_size("gx"),
        lax.axis_size("gy"),
        lax.axis_size("gz"),
        span_first,
        span_second,
        span_third,
    )
    return blocks.transpose(0, 3, 1, 4, 2, 5).reshape(
        lax.axis_size("gx") * span_first,
        lax.axis_size("gy") * span_second,
        lax.axis_size("gz") * span_third,
    )


def edge_factors(length, offset, whole_length, lower_flag, upper_flag):
    position = jnp.arange(length, dtype=jnp.int32) + offset
    lower = jnp.where(position == 0, lower_flag.astype(jnp.float32), jnp.float32(1.0))
    upper = jnp.where(
        position == whole_length - 1, upper_flag.astype(jnp.float32), jnp.float32(1.0)
    )
    return (lower, upper)


def coefficients(padded_density, factors, weight):
    centre = padded_density[1:-1, 1:-1, 1:-1]
    following = (
        padded_density[2:, 1:-1, 1:-1],
        padded_density[1:-1, 2:, 1:-1],
        padded_density[1:-1, 1:-1, 2:],
    )
    preceding = (
        padded_density[:-2, 1:-1, 1:-1],
        padded_density[1:-1, :-2, 1:-1],
        padded_density[1:-1, 1:-1, :-2],
    )
    upper_coefs = tuple(
        (
            weight
            * 2.0
            / (centre + following[direction])
            * factors[direction][1].reshape(SHAPES[direction])
            for direction in range(3)
        )
    )
    lower_coefs = tuple(
        (
            weight
            * 2.0
            / (centre + preceding[direction])
            * factors[direction][0].reshape(SHAPES[direction])
            for direction in range(3)
        )
    )
    diagonal = (
        MASS_SHIFT
        + upper_coefs[0]
        + lower_coefs[0]
        + upper_coefs[1]
        + lower_coefs[1]
        + upper_coefs[2]
        + lower_coefs[2]
    )
    return (upper_coefs, lower_coefs, diagonal)


def neighbour_sum(padded_field, upper_coefs, lower_coefs):
    summed = (
        upper_coefs[0] * padded_field[2:, 1:-1, 1:-1]
        + lower_coefs[0] * padded_field[:-2, 1:-1, 1:-1]
    )
    summed = (
        summed
        + upper_coefs[1] * padded_field[1:-1, 2:, 1:-1]
        + lower_coefs[1] * padded_field[1:-1, :-2, 1:-1]
    )
    summed = (
        summed
        + upper_coefs[2] * padded_field[1:-1, 1:-1, 2:]
        + lower_coefs[2] * padded_field[1:-1, 1:-1, :-2]
    )
    return summed


def apply_level(field, level_data):
    return level_data[3] * field - neighbour_sum(level_data[0](field), level_data[1], level_data[2])


def smooth_once(iterate, source, level_data):
    return iterate + RELAXATION * (source - apply_level(iterate, level_data)) / level_data[3]


def relax_from_zero(source, level_data, sweeps_count):
    iterate = RELAXATION * source / level_data[3]
    for repeat in range(sweeps_count - 1):
        iterate = smooth_once(iterate, source, level_data)
    return iterate


def restrict(field):
    span_first, span_second, span_third = field.shape
    return field.reshape(span_first // 2, 2, span_second // 2, 2, span_third // 2, 2).mean(
        axis=(1, 3, 5)
    )


def prolong(field):
    span_first, span_second, span_third = field.shape
    spread = jnp.broadcast_to(
        field[:, None, :, None, :, None], (span_first, 2, span_second, 2, span_third, 2)
    )
    return spread.reshape(2 * span_first, 2 * span_second, 2 * span_third)


def deep_cycle(source, extended_levels, coarse_solve):
    extended = extended_levels[0]
    source_ext = deep_padded(source)
    iterate = RELAXATION * source_ext / extended[3]
    width = SWEEPS
    for repeat in range(SWEEPS - 1):
        iterate = sweep_inner(iterate, source_ext, extended, width)
        width = width - 1
    margin = SWEEPS - (width - 1)
    residue = trimmed(source_ext, margin) - apply_inner(iterate, extended, width)
    iterate = trimmed(iterate, width)
    if len(extended_levels) > 1:
        correction = deep_cycle(restrict(residue), extended_levels[1:], coarse_solve)
    else:
        correction = coarse_solve(restrict(residue))
    iterate = deep_padded(iterate + prolong(correction))
    width = SWEEPS
    for repeat in range(SWEEPS):
        iterate = sweep_inner(iterate, source_ext, extended, width)
        width = width - 1
    return iterate


def deep_solve(source, levels, extended_levels, coarse_solve):
    iterate = deep_cycle(source, extended_levels, coarse_solve)
    iterate = iterate + deep_cycle(
        source - apply_level(iterate, levels[0]), extended_levels, coarse_solve
    )
    return iterate


def divergence(fluxes, padder):
    first = padder(fluxes[0])[:-2, 1:-1, 1:-1]
    second = padder(fluxes[1])[1:-1, :-2, 1:-1]
    third = padder(fluxes[2])[1:-1, 1:-1, :-2]
    return fluxes[0] - first + (fluxes[1] - second) + (fluxes[2] - third)


def upward_differences(field, padder):
    padded = padder(field)
    return (
        padded[2:, 1:-1, 1:-1] - field,
        padded[1:-1, 2:, 1:-1] - field,
        padded[1:-1, 1:-1, 2:] - field,
    )


def closure_plane(feature_plane, weight_in, bias_in, weight_out):
    columns = feature_plane.reshape(feature_plane.shape[0], -1)
    before = jnp.dot(weight_in.T, columns, preferred_element_type=jnp.float32) + bias_in[:, None]
    gate = jax.nn.sigmoid(before)
    hidden = (before * gate).astype(jnp.bfloat16)
    output = jnp.dot(weight_out.T, hidden, preferred_element_type=jnp.float32)
    return output.reshape((3,) + feature_plane.shape[1:])


def closure_field(features, weight_in, bias_in, weight_out):

    def one_plane(index):
        feature_plane = lax.dynamic_index_in_dim(features, index, 1, keepdims=False)
        return closure_plane(feature_plane, weight_in, bias_in, weight_out)

    stacked = lax.map(one_plane, jnp.arange(features.shape[1], dtype=jnp.int32))
    return jnp.moveaxis(stacked, 0, 1)


def gradient_plane(totals, feature_plane, grad_plane, weight_in, bias_in, weight_out):
    columns = feature_plane.reshape(feature_plane.shape[0], -1)
    before = jnp.dot(weight_in.T, columns, preferred_element_type=jnp.float32) + bias_in[:, None]
    gate = jax.nn.sigmoid(before)
    hidden = (before * gate).astype(jnp.bfloat16)
    upstream = grad_plane.reshape(3, -1).astype(jnp.bfloat16)
    grad_out = lax.dot_general(
        hidden, upstream, (((1,), (1,)), ((), ())), preferred_element_type=jnp.float32
    )
    grad_hidden = jnp.dot(weight_out, upstream, preferred_element_type=jnp.float32)
    grad_before = grad_hidden * (gate * (1.0 + before * (1.0 - gate)))
    grad_bias = jnp.sum(grad_before, axis=1)
    grad_in = lax.dot_general(
        columns,
        grad_before.astype(jnp.bfloat16),
        (((1,), (1,)), ((), ())),
        preferred_element_type=jnp.float32,
    )
    return (totals[0] + grad_in, totals[1] + grad_bias, totals[2] + grad_out)


def closure_gradients(features, grad_correction, weight_in, bias_in, weight_out):

    def step_plane(totals, index):
        feature_plane = lax.dynamic_index_in_dim(features, index, 1, keepdims=False)
        grad_plane = lax.dynamic_index_in_dim(grad_correction, index, 1, keepdims=False)
        return (
            gradient_plane(totals, feature_plane, grad_plane, weight_in, bias_in, weight_out),
            None,
        )

    start = (
        jnp.zeros(weight_in.shape, jnp.float32),
        jnp.zeros(bias_in.shape, jnp.float32),
        jnp.zeros(weight_out.shape, jnp.float32),
    )
    totals, unused = lax.scan(step_plane, start, jnp.arange(features.shape[1], dtype=jnp.int32))
    return totals


def training_step(
    velocity,
    features,
    target,
    weight_in,
    bias_in,
    weight_out,
    levels,
    solver,
    fine_factors,
    cells_total,
):
    padder = levels[0][0]
    upper_coefs = levels[0][1]
    outlets = tuple(
        (fine_factors[direction][1].reshape(SHAPES[direction]) for direction in range(3))
    )
    correction = closure_field(features, weight_in, bias_in, weight_out)
    fluxes = tuple(
        (
            (velocity[direction] + correction[direction]) * outlets[direction]
            for direction in range(3)
        )
    )
    source = -divergence(fluxes, padder)
    pressure = solver(source)
    rises = upward_differences(pressure, padder)
    new_velocity = jnp.stack(
        [fluxes[direction] - upper_coefs[direction] * rises[direction] for direction in range(3)]
    )
    misfit = (new_velocity - target) / cells_total
    weighted = tuple((upper_coefs[direction] * misfit[direction] for direction in range(3)))
    grad_pressure = divergence(weighted, padder)
    grad_source = solver(grad_pressure)
    drops = upward_differences(grad_source, padder)
    grad_correction = jnp.stack(
        [(misfit[direction] + drops[direction]) * outlets[direction] for direction in range(3)]
    )
    totals = closure_gradients(features, grad_correction, weight_in, bias_in, weight_out)
    return (new_velocity, totals)


def per_device(velocity, features, density, target, weight_in, bias_in, weight_out, open_faces):
    counts = (lax.axis_size("gx"), lax.axis_size("gy"), lax.axis_size("gz"))
    indices = (lax.axis_index("gx"), lax.axis_index("gy"), lax.axis_index("gz"))

    def level_factors(shape_now):
        return tuple(
            (
                edge_factors(
                    shape_now[direction],
                    indices[direction] * shape_now[direction],
                    shape_now[direction] * counts[direction],
                    open_faces[2 * direction],
                    open_faces[2 * direction + 1],
                )
                for direction in range(3)
            )
        )

    def make_level(level_density, weight):
        upper_coefs, lower_coefs, diagonal = coefficients(
            halo_padded(level_density), level_factors(level_density.shape), weight
        )
        return (halo_padded, upper_coefs, lower_coefs, diagonal)

    density_one = restrict(density)
    density_two = restrict(density_one)
    levels = (make_level(density, 1.0), make_level(density_one, 0.25))
    whole_density = gather_whole(density_two)
    whole_factors = tuple(
        (
            edge_factors(
                whole_density.shape[direction],
                0,
                whole_density.shape[direction],
                open_faces[2 * direction],
                open_faces[2 * direction + 1],
            )
            for direction in range(3)
        )
    )
    whole_upper, whole_lower, whole_diagonal = coefficients(
        zero_padded(whole_density), whole_factors, 0.0625
    )
    coarse_level = (zero_padded, whole_upper, whole_lower, whole_diagonal)

    def coarse_solve(source):
        whole_source = gather_whole(source)
        whole_iterate = relax_from_zero(whole_source, coarse_level, COARSE_SWEEPS)
        starts = tuple((indices[direction] * source.shape[direction] for direction in range(3)))
        return lax.dynamic_slice(whole_iterate, starts, source.shape)

    extended_levels = tuple((deep_coefs(level_data) for level_data in levels))

    def solver(source):
        return deep_solve(source, levels, extended_levels, coarse_solve)

    cells_total = density.size * counts[0] * counts[1] * counts[2]
    new_velocity, totals = training_step(
        velocity,
        features,
        target,
        weight_in,
        bias_in,
        weight_out,
        levels,
        solver,
        level_factors(density.shape),
        cells_total,
    )
    summed = lax.psum((totals[0], totals[1], totals[2]), ("gx", "gy", "gz"))
    return (new_velocity, summed[0], summed[1], summed[2])


F32 = jnp.float32
BF16 = jnp.bfloat16
MSG = 11
VMEM_BYTES = 56 * 1024 * 1024


def iota(shape, dim):
    return lax.broadcasted_iota(jnp.int32, shape, dim)


def ahead(plane, step, dim):
    return pltpu.roll(plane, plane.shape[dim] - step, dim)


def behind(plane, step, dim):
    return pltpu.roll(plane, step, dim)


def write_message(msg_ref, fields, sign):
    first, second, third = fields
    span, rows, lanes = first.shape
    row = iota((rows, lanes), 0)
    lane = iota((rows, lanes), 1)
    second_face = jnp.zeros((rows, lanes), F32)
    third_face = jnp.zeros((rows, lanes), F32)
    for x in range(span):
        total = first[x] + second[x] + third[x]
        if x > 0:
            total = total - first[x - 1]
        total = total - jnp.where(row == 0, 0.0, behind(second[x], 1, 0))
        total = total - jnp.where(lane == 0, 0.0, behind(third[x], 1, 1))
        msg_ref[x] = sign * total
        second_face = jnp.where(row == x, behind(second[x], x + 1, 0) if x < rows - 1 else second[x], second_face)
        third_face = jnp.where(lane == x, behind(third[x], x + 1, 1), third_face)
    msg_ref[span] = -sign * first[span - 1]
    msg_ref[span + 1] = -sign * second_face
    msg_ref[span + 2] = -sign * third_face


def local_outlets(open_ref, counts, shape):
    span, rows, lanes = shape
    here = [lax.axis_index(name) == count - 1 for name, count in zip(("gx", "gy", "gz"), counts)]
    one = jnp.float32(1.0)
    ends = [jnp.where(here[d], open_ref[2 * d + 1], one) for d in range(3)]
    row = iota((rows, lanes), 0)
    lane = iota((rows, lanes), 1)
    second = jnp.where(row == rows - 1, ends[1], one)
    third = jnp.where(lane == lanes - 1, ends[2], one)
    return ends[0], second, third


def forward_kernel(counts, open_ref, cols_ref, vel_ref, win_ref, bias_ref, wout_ref, flux_ref, msg_ref, corr):
    _, span, rows, lanes = vel_ref.shape
    chunk = rows * lanes
    for x in range(span):
        before = jnp.dot(win_ref[...], cols_ref[:, x * chunk : (x + 1) * chunk], preferred_element_type=F32)
        before = before + bias_ref[...]
        hidden = (before * jax.nn.sigmoid(before)).astype(BF16)
        out = jnp.dot(wout_ref[...], hidden, preferred_element_type=F32)
        for d in range(3):
            for y in range(rows):
                corr[d, x, y : y + 1, :] = out[d : d + 1, y * lanes : (y + 1) * lanes]
    first_end, second, third = local_outlets(open_ref, counts, (span, rows, lanes))
    fields = []
    for d in range(3):
        planes = []
        for x in range(span):
            plane = vel_ref[d, x] + corr[d, x]
            if d == 0:
                plane = plane * first_end if x == span - 1 else plane
            else:
                plane = plane * (second if d == 1 else third)
            flux_ref[d, x] = plane
            planes.append(plane)
        fields.append(jnp.stack(planes))
    write_message(msg_ref, fields, -1.0)


class Level:
    pass


def pair_sum(plane, step):
    rows, lanes = plane.shape
    row = iota((rows, lanes), 0)
    lane = iota((rows, lanes), 1)
    odd = lax.rem(row // step, 2) == 1
    plane = plane + jnp.where(odd, behind(plane, step, 0), ahead(plane, step, 0))
    odd = lax.rem(lane // step, 2) == 1
    return plane + jnp.where(odd, behind(plane, step, 1), ahead(plane, step, 1))


def raw_upper(level, open_ref, x):
    rows, lanes = level.rho.shape[1:]
    row = iota((rows, lanes), 0)
    lane = iota((rows, lanes), 1)
    step = level.step
    rho = level.rho[x + 1]
    last_row = row >= rows - step
    last_lane = lane >= lanes - step
    one = jnp.float32(1.0)
    up0 = jnp.where(x == level.span - 1, open_ref[1], one) * (2.0 * level.weight) / (rho + level.rho[x + 2])
    up1 = (2.0 * level.weight) / (rho + jnp.where(last_row, 0.0, ahead(rho, step, 0)))
    up1 = up1 * jnp.where(last_row, open_ref[3], one)
    up2 = (2.0 * level.weight) / (rho + jnp.where(last_lane, 0.0, ahead(rho, step, 1)))
    up2 = up2 * jnp.where(last_lane, open_ref[5], one)
    return up0, up1, up2


def build_level(level, open_ref):
    rows, lanes = level.rho.shape[1:]
    step = level.step

    def body(x, unused):
        row = iota((rows, lanes), 0)
        lane = iota((rows, lanes), 1)
        one = jnp.float32(1.0)
        rho = level.rho[x + 1]
        up0, up1, up2 = raw_upper(level, open_ref, x)
        twice = 2.0 * level.weight
        down0 = jnp.where(x == 0, open_ref[0], one) * twice / (rho + level.rho[x])
        first_row = row < step
        first_lane = lane < step
        down1 = jnp.where(first_row, open_ref[2] * twice / rho, behind(up1, step, 0))
        down2 = jnp.where(first_lane, open_ref[4] * twice / rho, behind(up2, step, 1))
        diagonal = MASS_SHIFT + up0 + down0 + up1 + down1 + up2 + down2
        scale = RELAXATION / diagonal
        level.scale[x] = scale
        level.unscale[x] = diagonal * (1.0 / RELAXATION)
        level.coef[0, x] = scale * up0
        level.coef[1, x] = scale * down0
        level.coef[2, x] = jnp.where(row >= rows - step, 0.0, scale * up1)
        level.coef[3, x] = jnp.where(first_row, 0.0, scale * down1)
        level.coef[4, x] = jnp.where(lane >= lanes - step, 0.0, scale * up2)
        level.coef[5, x] = jnp.where(first_lane, 0.0, scale * down2)
        return unused

    lax.fori_loop(0, level.span, body, 0)


def smoothed(level, src, scaled, x):
    step = level.step
    mid = src[x + 1]
    total = scaled[x + 1] + (1.0 - RELAXATION) * mid
    total = total + (level.coef[0, x] * src[x + 2] + level.coef[1, x] * src[x])
    total = total + (level.coef[2, x] * ahead(mid, step, 0) + level.coef[3, x] * behind(mid, step, 0))
    return total + (level.coef[4, x] * ahead(mid, step, 1) + level.coef[5, x] * behind(mid, step, 1))


def loop(count, body):
    def step(x, unused):
        body(x)
        return unused

    lax.fori_loop(0, count, step, 0, unroll=2)


def sweep(level, src, dst, scaled):
    def body(x):
        dst[x + 1] = smoothed(level, src, scaled, x)

    loop(level.span, body)


def cycle(levels, scaled, one, two):
    level = levels[0]
    if len(levels) == 1:
        src, dst, spare = scaled, one, two
        for repeat in range(COARSE_SWEEPS - 1):
            sweep(level, src, dst, scaled)
            src, dst, spare = dst, spare, dst
        return src
    sweep(level, scaled, one, scaled)
    src, dst = one, two
    for repeat in range(SWEEPS - 2):
        sweep(level, src, dst, scaled)
        src, dst = dst, src
    below = levels[1]

    def lower(x):
        even = (smoothed(level, src, scaled, 2 * x) - src[2 * x + 1]) * level.unscale[2 * x]
        odd = (smoothed(level, src, scaled, 2 * x + 1) - src[2 * x + 2]) * level.unscale[2 * x + 1]
        below.scaled[x + 1] = pair_sum(even + odd, level.step) * 0.125 * below.scale[x]

    lax.fori_loop(0, below.span, lambda x, unused: (lower(x), unused)[1], 0)
    coarse = cycle(levels[1:], below.scaled, below.one, below.two)

    def raise_(x):
        extra = coarse[x + 1]
        src[2 * x + 1] = src[2 * x + 1] + extra
        src[2 * x + 2] = src[2 * x + 2] + extra

    loop(below.span, raise_)
    for repeat in range(SWEEPS):
        sweep(level, src, dst, scaled)
        src, dst = dst, src
    return src


def make_levels(refs):
    levels = []
    for depth in range(3):
        level = Level()
        level.step = 2**depth
        level.weight = 0.25**depth
        level.rho, level.scale, level.unscale, level.coef, level.scaled, level.one, level.two = refs[7 * depth : 7 * depth + 7]
        level.span = level.scale.shape[0]
        levels.append(level)
    return levels


def level_scratch(whole):
    shapes = []
    for depth in range(3):
        span = whole[0] // 2**depth
        plane = tuple(whole[1:])
        padded = pltpu.VMEM((span + 2,) + plane, F32)
        flat = pltpu.VMEM((span,) + plane, F32)
        shapes += [padded, flat, flat, pltpu.VMEM((6, span) + plane, F32), padded, padded, padded]
    return shapes


def clear_ends(ref):
    zero = jnp.zeros(ref.shape[1:], F32)
    ref[0] = zero
    ref[ref.shape[0] - 1] = zero


def prepare(levels, open_ref, density_ref, counts):
    blocks, span, rows, lanes = density_ref.shape
    for level in levels:
        for ref in (level.rho, level.scaled, level.one, level.two):
            clear_ends(ref)
    for i in range(counts[0]):
        for j in range(counts[1]):
            for k in range(counts[2]):
                block = (i * counts[1] + j) * counts[2] + k
                levels[0].rho[
                    1 + span * i : 1 + span * (i + 1), rows * j : rows * (j + 1), lanes * k : lanes * (k + 1)
                ] = density_ref[block]
    for level, below in zip(levels[:-1], levels[1:]):

        def body(x, level=level, below=below):
            below.rho[x + 1] = pair_sum(level.rho[2 * x + 1] + level.rho[2 * x + 2], level.step) * 0.125

        loop(below.span, body)
    for level in levels:
        build_level(level, open_ref)


def assemble(target, msg_ref, counts):
    blocks, planes, rows, lanes = msg_ref.shape
    span = planes - 3
    lane = iota((rows, lanes), 1)
    for i in range(counts[0]):
        for j in range(counts[1]):
            for k in range(counts[2]):
                block = (i * counts[1] + j) * counts[2] + k
                at_rows = slice(rows * j, rows * (j + 1))
                at_lanes = slice(lanes * k, lanes * (k + 1))
                for x in range(span):
                    plane = msg_ref[block, x]
                    if x == 0 and i > 0:
                        plane = plane + msg_ref[block - counts[1] * counts[2], span]
                    if k > 0:
                        face = msg_ref[block - 1, span + 2]
                        face = ahead(face, x, 1) if x > 0 else face
                        plane = plane + jnp.where(lane == 0, face, 0.0)
                    target[1 + span * i + x, at_rows, at_lanes] = plane
                    if j > 0:
                        face = msg_ref[block - counts[2], span + 1, x : x + 1, :]
                        at_row = slice(rows * j, rows * j + 1)
                        target[1 + span * i + x, at_row, at_lanes] = (
                            target[1 + span * i + x, at_row, at_lanes] + face
                        )


def solve(levels, msg_ref, counts, kept):
    fine = levels[0]
    assemble(fine.scaled, msg_ref, counts)

    def scale(x):
        fine.scaled[x + 1] = fine.scaled[x + 1] * fine.scale[x]

    loop(fine.span, scale)
    first = cycle(levels, fine.scaled, fine.one, fine.two)

    def again(x):
        mid = first[x + 1]
        kept[x + 1] = mid
        fine.again[x + 1] = smoothed(fine, first, fine.scaled, x) - mid

    loop(fine.span, again)
    second = cycle(levels, fine.again, fine.one, fine.two)

    def add(x):
        kept[x + 1] = kept[x + 1] + second[x + 1]

    loop(fine.span, add)


def rises(kept, wide, slot, start, span):
    rows, lanes = kept.shape[1:]

    def body(x, unused):
        row = iota((rows, lanes), 0)
        lane = iota((rows, lanes), 1)
        mid = kept[start + x + 1]
        wide[slot, x] = kept[start + x + 2] - mid
        wide[slot + 1, x] = jnp.where(row == rows - 1, 0.0, ahead(mid, 1, 0)) - mid
        wide[slot + 2, x] = jnp.where(lane == lanes - 1, 0.0, ahead(mid, 1, 1)) - mid
        return unused

    lax.fori_loop(0, span, body, 0)


def own_block(wide, slot, rows, lanes):
    j = lax.axis_index("gy")
    k = lax.axis_index("gz")
    return wide[slot, :, pl.ds(pl.multiple_of(j * rows, rows), rows), pl.ds(pl.multiple_of(k * lanes, lanes), lanes)]


def project_kernel(counts, open_ref, density_ref, msg_ref, flux_ref, target_ref, new_ref, misfit_ref, out_ref, kept, extra, wide, *refs):
    levels = make_levels(refs)
    fine = levels[0]
    fine.again = extra
    clear_ends(kept)
    clear_ends(extra)
    prepare(levels, open_ref, density_ref, counts)
    solve(levels, msg_ref, counts, kept)
    _, span, rows, lanes = flux_ref.shape
    start = lax.axis_index("gx") * span
    rises(kept, wide, 0, start, span)

    def body(x, unused):
        ups = raw_upper(fine, open_ref, start + x)
        for d in range(3):
            wide[3 + d, x] = ups[d]
        return unused

    lax.fori_loop(0, span, body, 0)
    cells = counts[0] * counts[1] * counts[2] * span * rows * lanes
    fields = []
    for d in range(3):
        upper = own_block(wide, 3 + d, rows, lanes)
        fresh = flux_ref[d] - upper * own_block(wide, d, rows, lanes)
        new_ref[d] = fresh
        misfit = (fresh - target_ref[d]) / cells
        misfit_ref[d] = misfit
        fields.append(upper * misfit)
    write_message(out_ref, fields, 1.0)


def adjoint_kernel(counts, open_ref, density_ref, msg_ref, misfit_ref, cols_ref, win_ref, bias_ref, wout_ref, out_ref, upstream, kept, extra, wide, *refs):
    levels = make_levels(refs)
    fine = levels[0]
    fine.again = extra
    clear_ends(kept)
    clear_ends(extra)
    prepare(levels, open_ref, density_ref, counts)
    solve(levels, msg_ref, counts, kept)
    _, span, rows, lanes = misfit_ref.shape
    start = lax.axis_index("gx") * span
    rises(kept, wide, 0, start, span)
    first_end, second, third = local_outlets(open_ref, counts, (span, rows, lanes))
    chunk = rows * lanes
    upstream[...] = jnp.zeros(upstream.shape, F32)
    for d in range(3):
        block = misfit_ref[d] + own_block(wide, d, rows, lanes)
        for x in range(span):
            plane = block[x]
            if d == 0:
                plane = plane * first_end if x == span - 1 else plane
            else:
                plane = plane * (second if d == 1 else third)
            for y in range(rows):
                upstream[d : d + 1, x * chunk + y * lanes : x * chunk + (y + 1) * lanes] = plane[y : y + 1]
    across = (((1,), (1,)), ((), ()))
    hidden_size = win_ref.shape[0]
    feat = win_ref.shape[1]
    grad_in = jnp.zeros((feat, hidden_size), F32)
    grad_out = jnp.zeros((8, hidden_size), F32)
    grad_bias = jnp.zeros((8, hidden_size), F32)
    ones = jnp.ones((8, chunk), BF16)
    for x in range(span):
        columns = cols_ref[:, x * chunk : (x + 1) * chunk]
        before = jnp.dot(win_ref[...], columns, preferred_element_type=F32) + bias_ref[...]
        gate = jax.nn.sigmoid(before)
        hidden = (before * gate).astype(BF16)
        up = upstream[:, x * chunk : (x + 1) * chunk].astype(BF16)
        grad_out = grad_out + lax.dot_general(up, hidden, across, preferred_element_type=F32)
        grad_hidden = lax.dot_general(wout_ref[...], up, (((0,), (0,)), ((), ())), preferred_element_type=F32)
        grad_before = grad_hidden * (gate * (1.0 + before * (1.0 - gate)))
        high = grad_before.astype(BF16)
        low = (grad_before - high.astype(F32)).astype(BF16)
        grad_bias = grad_bias + lax.dot_general(ones, high, across, preferred_element_type=F32)
        grad_bias = grad_bias + lax.dot_general(ones, low, across, preferred_element_type=F32)
        grad_in = grad_in + lax.dot_general(columns, high, across, preferred_element_type=F32)
    out_ref[0:feat, :] = grad_in
    out_ref[feat : feat + 8, :] = grad_out
    out_ref[feat + 8 : feat + 16, :] = grad_bias


def whole_device(counts, velocity, features, density, target, weight_in, bias_in, weight_out, open_faces):
    axes = ("gx", "gy", "gz")
    shape = density.shape
    span, rows, lanes = shape
    whole = tuple(n * c for n, c in zip(shape, counts))
    feat, hidden_size = weight_in.shape
    cells = span * rows * lanes
    opens = open_faces.astype(F32)
    columns = features.reshape(feat, cells)
    win = weight_in.T
    bias = bias_in.reshape(hidden_size, 1)
    wout = jnp.pad(weight_out.T, ((0, 5), (0, 0)))
    vmem = pl.BlockSpec(memory_space=pltpu.VMEM)
    smem = pl.BlockSpec(memory_space=pltpu.SMEM)
    params = pltpu.CompilerParams(vmem_limit_bytes=VMEM_BYTES)
    blocks = lax.all_gather(density, axes, axis=0)
    field = jax.ShapeDtypeStruct((3,) + shape, F32)
    message = jax.ShapeDtypeStruct((span + 3, rows, lanes), F32)
    flux, msg = pl.pallas_call(
        functools.partial(forward_kernel, counts),
        out_shape=(field, message),
        in_specs=[smem] + [vmem] * 5,
        out_specs=(vmem, vmem),
        scratch_shapes=[pltpu.VMEM((3,) + shape, F32)],
        compiler_params=params,
        name="closure_forward",
    )(opens, columns, velocity, win, bias, wout)
    sources = lax.all_gather(msg, axes, axis=0)
    padded = pltpu.VMEM((whole[0] + 2,) + whole[1:], F32)
    wide = pltpu.VMEM((6, span) + whole[1:], F32)
    scratch = [padded, padded, wide] + level_scratch(whole)
    new_velocity, misfit, msg = pl.pallas_call(
        functools.partial(project_kernel, counts),
        out_shape=(field, field, message),
        in_specs=[smem] + [vmem] * 4,
        out_specs=(vmem, vmem, vmem),
        scratch_shapes=scratch,
        compiler_params=params,
        name="project",
    )(opens, blocks, sources, flux, target)
    sources = lax.all_gather(msg, axes, axis=0)
    sums = pl.pallas_call(
        functools.partial(adjoint_kernel, counts),
        out_shape=jax.ShapeDtypeStruct((feat + 16, hidden_size), F32),
        in_specs=[smem] + [vmem] * 7,
        out_specs=vmem,
        scratch_shapes=[pltpu.VMEM((8, cells), F32)] + scratch,
        compiler_params=params,
        name="adjoint",
    )(opens, blocks, sources, misfit, columns, win, bias, wout)
    sums = lax.psum(sums, axes)
    return new_velocity, sums[:feat], sums[feat + 8], sums[feat : feat + 3].T


def fits(mesh):
    return mesh.size <= 32


def solution(mesh):
    in_specs = (
        P(None, "gx", "gy", "gz"),
        P(None, "gx", "gy", "gz"),
        P("gx", "gy", "gz"),
        P(None, "gx", "gy", "gz"),
        P(),
        P(),
        P(),
        P(),
    )
    out_specs = (P(None, "gx", "gy", "gz"), P(), P(), P())
    counts = tuple(mesh.shape[name] for name in ("gx", "gy", "gz"))
    body = functools.partial(whole_device, counts) if fits(mesh) else per_device
    return jax.shard_map(
        body, mesh=mesh, in_specs=in_specs, out_specs=out_specs, check_vma=False
    )
```

```python
import functools

import jax
import jax.numpy as jnp
from jax import lax
from jax.experimental import pallas as pl
from jax.experimental.pallas import tpu as pltpu
from jax.sharding import PartitionSpec as P

SWEEPS = 3
COARSE_SWEEPS = 6


RELAXATION = 0.8
MASS_SHIFT = 0.05
SHAPES = ((-1, 1, 1), (1, -1, 1), (1, 1, -1))


def with_halo(shard, sides, width):
    for axis, dim in sides:
        count, length = (lax.axis_size(axis), shard.shape[dim])
        up = [(i, (i + 1) % count) for i in range(count - 1)]
        down = [(j, i) for i, j in up]
        last = lax.slice_in_dim(shard, length - width, length, axis=dim)
        leading = lax.slice_in_dim(shard, 0, width, axis=dim)
        before = lax.ppermute(last, axis, up)
        after = lax.ppermute(leading, axis, down)
        shard = jnp.concatenate([before, shard, after], axis=dim)
    return shard


def zero_padded(field):
    return jnp.pad(field, 1)


def halo_padded(field):
    return with_halo(field, (("gx", 0), ("gy", 1), ("gz", 2)), 1)


def deep_padded(field):
    return with_halo(field, (("gx", 0), ("gy", 1), ("gz", 2)), SWEEPS)


def deep_coefs(level_data):
    stacked = jnp.stack(list(level_data[1]) + list(level_data[2]) + [level_data[3]])
    extended = with_halo(stacked, (("gx", 1), ("gy", 2), ("gz", 3)), SWEEPS)
    diagonal = extended[6]
    safe_diagonal = jnp.where(diagonal > 0.0, diagonal, jnp.float32(1.0))
    return (
        (extended[0], extended[1], extended[2]),
        (extended[3], extended[4], extended[5]),
        diagonal,
        safe_diagonal,
    )


def trimmed(field, margin):
    span_first, span_second, span_third = field.shape
    return field[
        margin : span_first - margin, margin : span_second - margin, margin : span_third - margin
    ]


def apply_inner(iterate, extended, width):
    margin = SWEEPS - (width - 1)
    uppers = tuple((trimmed(extended[0][direction], margin) for direction in range(3)))
    lowers = tuple((trimmed(extended[1][direction], margin) for direction in range(3)))
    diagonal = trimmed(extended[2], margin)
    summed = neighbour_sum(iterate, uppers, lowers)
    return diagonal * iterate[1:-1, 1:-1, 1:-1] - summed


def sweep_inner(iterate, source_ext, extended, width):
    margin = SWEEPS - (width - 1)
    residue = trimmed(source_ext, margin) - apply_inner(iterate, extended, width)
    return iterate[1:-1, 1:-1, 1:-1] + RELAXATION * residue / trimmed(extended[3], margin)


def gather_whole(coarse_piece):
    span_first, span_second, span_third = coarse_piece.shape
    flattened = coarse_piece.reshape(1, span_first * span_second * span_third)
    gathered = lax.all_gather(flattened, ("gx", "gy", "gz"), axis=0, tiled=True)
    blocks = gathered.reshape(
        lax.axis_size("gx"),
        lax.axis_size("gy"),
        lax.axis_size("gz"),
        span_first,
        span_second,
        span_third,
    )
    return blocks.transpose(0, 3, 1, 4, 2, 5).reshape(
        lax.axis_size("gx") * span_first,
        lax.axis_size("gy") * span_second,
        lax.axis_size("gz") * span_third,
    )


def edge_factors(length, offset, whole_length, lower_flag, upper_flag):
    position = jnp.arange(length, dtype=jnp.int32) + offset
    lower = jnp.where(position == 0, lower_flag.astype(jnp.float32), jnp.float32(1.0))
    upper = jnp.where(
        position == whole_length - 1, upper_flag.astype(jnp.float32), jnp.float32(1.0)
    )
    return (lower, upper)


def coefficients(padded_density, factors, weight):
    centre = padded_density[1:-1, 1:-1, 1:-1]
    following = (
        padded_density[2:, 1:-1, 1:-1],
        padded_density[1:-1, 2:, 1:-1],
        padded_density[1:-1, 1:-1, 2:],
    )
    preceding = (
        padded_density[:-2, 1:-1, 1:-1],
        padded_density[1:-1, :-2, 1:-1],
        padded_density[1:-1, 1:-1, :-2],
    )
    upper_coefs = tuple(
        (
            weight
            * 2.0
            / (centre + following[direction])
            * factors[direction][1].reshape(SHAPES[direction])
            for direction in range(3)
        )
    )
    lower_coefs = tuple(
        (
            weight
            * 2.0
            / (centre + preceding[direction])
            * factors[direction][0].reshape(SHAPES[direction])
            for direction in range(3)
        )
    )
    diagonal = (
        MASS_SHIFT
        + upper_coefs[0]
        + lower_coefs[0]
        + upper_coefs[1]
        + lower_coefs[1]
        + upper_coefs[2]
        + lower_coefs[2]
    )
    return (upper_coefs, lower_coefs, diagonal)


def neighbour_sum(padded_field, upper_coefs, lower_coefs):
    summed = (
        upper_coefs[0] * padded_field[2:, 1:-1, 1:-1]
        + lower_coefs[0] * padded_field[:-2, 1:-1, 1:-1]
    )
    summed = (
        summed
        + upper_coefs[1] * padded_field[1:-1, 2:, 1:-1]
        + lower_coefs[1] * padded_field[1:-1, :-2, 1:-1]
    )
    summed = (
        summed
        + upper_coefs[2] * padded_field[1:-1, 1:-1, 2:]
        + lower_coefs[2] * padded_field[1:-1, 1:-1, :-2]
    )
    return summed


def apply_level(field, level_data):
    return level_data[3] * field - neighbour_sum(level_data[0](field), level_data[1], level_data[2])


def smooth_once(iterate, source, level_data):
    return iterate + RELAXATION * (source - apply_level(iterate, level_data)) / level_data[3]


def relax_from_zero(source, level_data, sweeps_count):
    iterate = RELAXATION * source / level_data[3]
    for repeat in range(sweeps_count - 1):
        iterate = smooth_once(iterate, source, level_data)
    return iterate


def restrict(field):
    span_first, span_second, span_third = field.shape
    return field.reshape(span_first // 2, 2, span_second // 2, 2, span_third // 2, 2).mean(
        axis=(1, 3, 5)
    )


def prolong(field):
    span_first, span_second, span_third = field.shape
    spread = jnp.broadcast_to(
        field[:, None, :, None, :, None], (span_first, 2, span_second, 2, span_third, 2)
    )
    return spread.reshape(2 * span_first, 2 * span_second, 2 * span_third)


def deep_cycle(source, extended_levels, coarse_solve):
    extended = extended_levels[0]
    source_ext = deep_padded(source)
    iterate = RELAXATION * source_ext / extended[3]
    width = SWEEPS
    for repeat in range(SWEEPS - 1):
        iterate = sweep_inner(iterate, source_ext, extended, width)
        width = width - 1
    margin = SWEEPS - (width - 1)
    residue = trimmed(source_ext, margin) - apply_inner(iterate, extended, width)
    iterate = trimmed(iterate, width)
    if len(extended_levels) > 1:
        correction = deep_cycle(restrict(residue), extended_levels[1:], coarse_solve)
    else:
        correction = coarse_solve(restrict(residue))
    iterate = deep_padded(iterate + prolong(correction))
    width = SWEEPS
    for repeat in range(SWEEPS):
        iterate = sweep_inner(iterate, source_ext, extended, width)
        width = width - 1
    return iterate


def deep_solve(source, levels, extended_levels, coarse_solve):
    iterate = deep_cycle(source, extended_levels, coarse_solve)
    iterate = iterate + deep_cycle(
        source - apply_level(iterate, levels[0]), extended_levels, coarse_solve
    )
    return iterate


def divergence(fluxes, padder):
    first = padder(fluxes[0])[:-2, 1:-1, 1:-1]
    second = padder(fluxes[1])[1:-1, :-2, 1:-1]
    third = padder(fluxes[2])[1:-1, 1:-1, :-2]
    return fluxes[0] - first + (fluxes[1] - second) + (fluxes[2] - third)


def upward_differences(field, padder):
    padded = padder(field)
    return (
        padded[2:, 1:-1, 1:-1] - field,
        padded[1:-1, 2:, 1:-1] - field,
        padded[1:-1, 1:-1, 2:] - field,
    )


def closure_plane(feature_plane, weight_in, bias_in, weight_out):
    columns = feature_plane.reshape(feature_plane.shape[0], -1)
    before = jnp.dot(weight_in.T, columns, preferred_element_type=jnp.float32) + bias_in[:, None]
    gate = jax.nn.sigmoid(before)
    hidden = (before * gate).astype(jnp.bfloat16)
    output = jnp.dot(weight_out.T, hidden, preferred_element_type=jnp.float32)
    return output.reshape((3,) + feature_plane.shape[1:])


def closure_field(features, weight_in, bias_in, weight_out):

    def one_plane(index):
        feature_plane = lax.dynamic_index_in_dim(features, index, 1, keepdims=False)
        return closure_plane(feature_plane, weight_in, bias_in, weight_out)

    stacked = lax.map(one_plane, jnp.arange(features.shape[1], dtype=jnp.int32))
    return jnp.moveaxis(stacked, 0, 1)


def gradient_plane(totals, feature_plane, grad_plane, weight_in, bias_in, weight_out):
    columns = feature_plane.reshape(feature_plane.shape[0], -1)
    before = jnp.dot(weight_in.T, columns, preferred_element_type=jnp.float32) + bias_in[:, None]
    gate = jax.nn.sigmoid(before)
    hidden = (before * gate).astype(jnp.bfloat16)
    upstream = grad_plane.reshape(3, -1).astype(jnp.bfloat16)
    grad_out = lax.dot_general(
        hidden, upstream, (((1,), (1,)), ((), ())), preferred_element_type=jnp.float32
    )
    grad_hidden = jnp.dot(weight_out, upstream, preferred_element_type=jnp.float32)
    grad_before = grad_hidden * (gate * (1.0 + before * (1.0 - gate)))
    grad_bias = jnp.sum(grad_before, axis=1)
    grad_in = lax.dot_general(
        columns,
        grad_before.astype(jnp.bfloat16),
        (((1,), (1,)), ((), ())),
        preferred_element_type=jnp.float32,
    )
    return (totals[0] + grad_in, totals[1] + grad_bias, totals[2] + grad_out)


def closure_gradients(features, grad_correction, weight_in, bias_in, weight_out):

    def step_plane(totals, index):
        feature_plane = lax.dynamic_index_in_dim(features, index, 1, keepdims=False)
        grad_plane = lax.dynamic_index_in_dim(grad_correction, index, 1, keepdims=False)
        return (
            gradient_plane(totals, feature_plane, grad_plane, weight_in, bias_in, weight_out),
            None,
        )

    start = (
        jnp.zeros(weight_in.shape, jnp.float32),
        jnp.zeros(bias_in.shape, jnp.float32),
        jnp.zeros(weight_out.shape, jnp.float32),
    )
    totals, unused = lax.scan(step_plane, start, jnp.arange(features.shape[1], dtype=jnp.int32))
    return totals


def training_step(
    velocity,
    features,
    target,
    weight_in,
    bias_in,
    weight_out,
    levels,
    solver,
    fine_factors,
    cells_total,
):
    padder = levels[0][0]
    upper_coefs = levels[0][1]
    outlets = tuple(
        (fine_factors[direction][1].reshape(SHAPES[direction]) for direction in range(3))
    )
    correction = closure_field(features, weight_in, bias_in, weight_out)
    fluxes = tuple(
        (
            (velocity[direction] + correction[direction]) * outlets[direction]
            for direction in range(3)
        )
    )
    source = -divergence(fluxes, padder)
    pressure = solver(source)
    rises = upward_differences(pressure, padder)
    new_velocity = jnp.stack(
        [fluxes[direction] - upper_coefs[direction] * rises[direction] for direction in range(3)]
    )
    misfit = (new_velocity - target) / cells_total
    weighted = tuple((upper_coefs[direction] * misfit[direction] for direction in range(3)))
    grad_pressure = divergence(weighted, padder)
    grad_source = solver(grad_pressure)
    drops = upward_differences(grad_source, padder)
    grad_correction = jnp.stack(
        [(misfit[direction] + drops[direction]) * outlets[direction] for direction in range(3)]
    )
    totals = closure_gradients(features, grad_correction, weight_in, bias_in, weight_out)
    return (new_velocity, totals)


def per_device(velocity, features, density, target, weight_in, bias_in, weight_out, open_faces):
    counts = (lax.axis_size("gx"), lax.axis_size("gy"), lax.axis_size("gz"))
    indices = (lax.axis_index("gx"), lax.axis_index("gy"), lax.axis_index("gz"))

    def level_factors(shape_now):
        return tuple(
            (
                edge_factors(
                    shape_now[direction],
                    indices[direction] * shape_now[direction],
                    shape_now[direction] * counts[direction],
                    open_faces[2 * direction],
                    open_faces[2 * direction + 1],
                )
                for direction in range(3)
            )
        )

    def make_level(level_density, weight):
        upper_coefs, lower_coefs, diagonal = coefficients(
            halo_padded(level_density), level_factors(level_density.shape), weight
        )
        return (halo_padded, upper_coefs, lower_coefs, diagonal)

    density_one = restrict(density)
    density_two = restrict(density_one)
    levels = (make_level(density, 1.0), make_level(density_one, 0.25))
    whole_density = gather_whole(density_two)
    whole_factors = tuple(
        (
            edge_factors(
                whole_density.shape[direction],
                0,
                whole_density.shape[direction],
                open_faces[2 * direction],
                open_faces[2 * direction + 1],
            )
            for direction in range(3)
        )
    )
    whole_upper, whole_lower, whole_diagonal = coefficients(
        zero_padded(whole_density), whole_factors, 0.0625
    )
    coarse_level = (zero_padded, whole_upper, whole_lower, whole_diagonal)

    def coarse_solve(source):
        whole_source = gather_whole(source)
        whole_iterate = relax_from_zero(whole_source, coarse_level, COARSE_SWEEPS)
        starts = tuple((indices[direction] * source.shape[direction] for direction in range(3)))
        return lax.dynamic_slice(whole_iterate, starts, source.shape)

    extended_levels = tuple((deep_coefs(level_data) for level_data in levels))

    def solver(source):
        return deep_solve(source, levels, extended_levels, coarse_solve)

    cells_total = density.size * counts[0] * counts[1] * counts[2]
    new_velocity, totals = training_step(
        velocity,
        features,
        target,
        weight_in,
        bias_in,
        weight_out,
        levels,
        solver,
        level_factors(density.shape),
        cells_total,
    )
    summed = lax.psum((totals[0], totals[1], totals[2]), ("gx", "gy", "gz"))
    return (new_velocity, summed[0], summed[1], summed[2])


F32 = jnp.float32
BF16 = jnp.bfloat16
MSG = 11
DOWN = (((0,), (0,)), ((), ()))
AXES = ("gx", "gy", "gz")
TILE = 128
VMEM_BYTES = 56 * 1024 * 1024


def opened(open_ref, face):
    return open_ref[face].astype(F32)


def iota(shape, dim):
    return lax.broadcasted_iota(jnp.int32, shape, dim)


def ahead(plane, step, dim):
    return pltpu.roll(plane, plane.shape[dim] - step, dim)


def behind(plane, step, dim):
    return pltpu.roll(plane, step, dim)


def write_message(msg_ref, fields, sign):
    first, second, third = fields
    span, rows, lanes = first.shape
    row = iota((rows, lanes), 0)
    lane = iota((rows, lanes), 1)
    second_face = jnp.zeros((rows, lanes), F32)
    third_face = jnp.zeros((rows, lanes), F32)
    for x in range(span):
        total = first[x] + second[x] + third[x]
        if x > 0:
            total = total - first[x - 1]
        total = total - jnp.where(row == 0, 0.0, behind(second[x], 1, 0))
        total = total - jnp.where(lane == 0, 0.0, behind(third[x], 1, 1))
        msg_ref[x] = sign * total
        second_face = jnp.where(row == x, behind(second[x], x + 1, 0) if x < rows - 1 else second[x], second_face)
        third_face = jnp.where(lane == x, behind(third[x], x + 1, 1), third_face)
    msg_ref[span] = -sign * first[span - 1]
    msg_ref[span + 1] = -sign * second_face
    msg_ref[span + 2] = -sign * third_face


def local_outlets(open_ref, counts, shape):
    span, rows, lanes = shape
    here = [lax.axis_index(name) == count - 1 for name, count in zip(("gx", "gy", "gz"), counts)]
    one = jnp.float32(1.0)
    ends = [jnp.where(here[d], opened(open_ref, 2 * d + 1), one) for d in range(3)]
    row = iota((rows, lanes), 0)
    lane = iota((rows, lanes), 1)
    second = jnp.where(row == rows - 1, ends[1], one)
    third = jnp.where(lane == lanes - 1, ends[2], one)
    return ends[0], second, third


def forward_kernel(counts, open_ref, cols_ref, vel_ref, win_ref, bias_ref, wout_ref, flux_ref, msg_ref, corr):
    _, span, rows, lanes = vel_ref.shape
    chunk = rows * lanes
    for x in range(span):
        before = lax.dot_general(win_ref[...], cols_ref[:, x * chunk : (x + 1) * chunk], DOWN, preferred_element_type=F32)
        before = before + bias_ref[...]
        hidden = (before * jax.nn.sigmoid(before)).astype(BF16)
        out = lax.dot_general(wout_ref[...], hidden, DOWN, preferred_element_type=F32)
        for d in range(3):
            for y in range(rows):
                corr[d, x, y : y + 1, :] = out[d : d + 1, y * lanes : (y + 1) * lanes]
    first_end, second, third = local_outlets(open_ref, counts, (span, rows, lanes))
    fields = []
    for d in range(3):
        planes = []
        for x in range(span):
            plane = vel_ref[d, x] + corr[d, x]
            if d == 0:
                plane = plane * first_end if x == span - 1 else plane
            else:
                plane = plane * (second if d == 1 else third)
            flux_ref[d, x] = plane
            planes.append(plane)
        fields.append(jnp.stack(planes))
    write_message(msg_ref, fields, -1.0)


class Level:
    pass


def exact_dot(values, ones):
    high = values.astype(BF16)
    low = (values - high.astype(F32)).astype(BF16)
    total = jnp.dot(high, ones, preferred_element_type=F32)
    return total + jnp.dot(low, ones, preferred_element_type=F32)


def pair_matrices(tools):
    gather, spread = tools[0], tools[1]
    for ref, fine, coarse in ((gather, 0, 1), (spread, 1, 0)):
        hit = iota(ref.shape, fine) // 2 == iota(ref.shape, coarse)
        ref[...] = jnp.where(hit, 1.0, 0.0).astype(BF16)


def block_means(tools, span, plane_of, put):
    gather, _, narrow, small, tall, _ = tools
    half = tall.shape[2] // 2

    def fold(x):
        plane = plane_of(x)
        for tile in range(tall.shape[1]):
            at = slice(tile * TILE, (tile + 1) * TILE)
            tall[x, tile] = plane[:, at]
            even = tall[x, tile, pl.ds(0, half, stride=2), :]
            odd = tall[x, tile, pl.ds(1, half, stride=2), :]
            narrow[pl.ds(pl.multiple_of(x * half, half), half), at] = even + odd

    loop(span, fold)
    small[...] = exact_dot(narrow[...], gather[...]) * 0.125

    def finish(x):
        put(x, small[pl.ds(pl.multiple_of(x * half, half), half), :])

    loop(span, finish)


def copy_to_fine(tools, span, coarse, put):
    _, spread, narrow, small, _, tall = tools
    half = tall.shape[2] // 2

    def pick(x):
        small[pl.ds(pl.multiple_of(x * half, half), half), :] = coarse[x + 1]

    loop(span, pick)
    narrow[...] = exact_dot(small[...], spread[...])

    def finish(x):
        rows = narrow[pl.ds(pl.multiple_of(x * half, half), half), :]
        for tile in range(tall.shape[1]):
            part = rows[:, tile * TILE : (tile + 1) * TILE]
            tall[x, tile, pl.ds(0, half, stride=2), :] = part
            tall[x, tile, pl.ds(1, half, stride=2), :] = part
        put(x, jnp.concatenate([tall[x, tile] for tile in range(tall.shape[1])], axis=1))

    loop(span, finish)


def pair_sum(plane, step):
    rows, lanes = plane.shape
    row = iota((rows, lanes), 0)
    lane = iota((rows, lanes), 1)
    odd = lax.rem(row // step, 2) == 1
    plane = plane + jnp.where(odd, behind(plane, step, 0), ahead(plane, step, 0))
    odd = lax.rem(lane // step, 2) == 1
    return plane + jnp.where(odd, behind(plane, step, 1), ahead(plane, step, 1))


def raw_upper(level, open_ref, x):
    rows, lanes = level.rho.shape[1:]
    row = iota((rows, lanes), 0)
    lane = iota((rows, lanes), 1)
    step = level.step
    rho = level.rho[x + 1]
    last_row = row >= rows - step
    last_lane = lane >= lanes - step
    one = jnp.float32(1.0)
    up0 = jnp.where(x == level.span - 1, opened(open_ref, 1), one) * (2.0 * level.weight) / (rho + level.rho[x + 2])
    up1 = (2.0 * level.weight) / (rho + jnp.where(last_row, 0.0, ahead(rho, step, 0)))
    up1 = up1 * jnp.where(last_row, opened(open_ref, 3), one)
    up2 = (2.0 * level.weight) / (rho + jnp.where(last_lane, 0.0, ahead(rho, step, 1)))
    up2 = up2 * jnp.where(last_lane, opened(open_ref, 5), one)
    return up0, up1, up2


def build_level(level, open_ref):
    rows, lanes = level.rho.shape[1:]
    step = level.step

    def body(x, unused):
        row = iota((rows, lanes), 0)
        lane = iota((rows, lanes), 1)
        one = jnp.float32(1.0)
        rho = level.rho[x + 1]
        up0, up1, up2 = raw_upper(level, open_ref, x)
        twice = 2.0 * level.weight
        down0 = jnp.where(x == 0, opened(open_ref, 0), one) * twice / (rho + level.rho[x])
        first_row = row < step
        first_lane = lane < step
        down1 = jnp.where(first_row, opened(open_ref, 2) * twice / rho, behind(up1, step, 0))
        down2 = jnp.where(first_lane, opened(open_ref, 4) * twice / rho, behind(up2, step, 1))
        diagonal = MASS_SHIFT + up0 + down0 + up1 + down1 + up2 + down2
        scale = RELAXATION / diagonal
        level.scale[x] = scale
        level.unscale[x] = diagonal * (1.0 / RELAXATION)
        level.coef[0, x] = scale * up0
        level.coef[1, x] = scale * down0
        level.coef[2, x] = jnp.where(row >= rows - step, 0.0, scale * up1)
        level.coef[3, x] = jnp.where(first_row, 0.0, scale * down1)
        level.coef[4, x] = jnp.where(lane >= lanes - step, 0.0, scale * up2)
        level.coef[5, x] = jnp.where(first_lane, 0.0, scale * down2)
        return unused

    lax.fori_loop(0, level.span, body, 0)


def smoothed(level, src, scaled, x):
    step = level.step
    mid = src[x + 1]
    total = scaled[x + 1] + (1.0 - RELAXATION) * mid
    total = total + (level.coef[0, x] * src[x + 2] + level.coef[1, x] * src[x])
    total = total + (level.coef[2, x] * ahead(mid, step, 0) + level.coef[3, x] * behind(mid, step, 0))
    return total + (level.coef[4, x] * ahead(mid, step, 1) + level.coef[5, x] * behind(mid, step, 1))


def loop(count, body):
    def step(x, unused):
        body(x)
        return unused

    lax.fori_loop(0, count, step, 0, unroll=4)


def sweep(level, src, dst, scaled):
    def body(x):
        dst[x + 1] = smoothed(level, src, scaled, x)

    loop(level.span, body)


def cycle(levels, scaled, one, two):
    level = levels[0]
    if len(levels) == 1:
        src, dst, spare = scaled, one, two
        for repeat in range(COARSE_SWEEPS - 1):
            sweep(level, src, dst, scaled)
            src, dst, spare = dst, spare, dst
        return src
    sweep(level, scaled, one, scaled)
    src, dst = one, two
    for repeat in range(SWEEPS - 2):
        sweep(level, src, dst, scaled)
        src, dst = dst, src
    below = levels[1]

    def lower(x):
        even = (smoothed(level, src, scaled, 2 * x) - src[2 * x + 1]) * level.unscale[2 * x]
        odd = (smoothed(level, src, scaled, 2 * x + 1) - src[2 * x + 2]) * level.unscale[2 * x + 1]
        return even + odd

    def store(x, mean):
        below.scaled[x + 1] = mean * below.scale[x]

    if level.tools is not None:
        block_means(level.tools, below.span, lower, store)
    else:
        loop(below.span, lambda x: store(x, pair_sum(lower(x), level.step) * 0.125))
    coarse = cycle(levels[1:], below.scaled, below.one, below.two)

    def raise_(x, extra):
        src[2 * x + 1] = src[2 * x + 1] + extra
        src[2 * x + 2] = src[2 * x + 2] + extra

    if level.tools is not None:
        copy_to_fine(level.tools, below.span, coarse, raise_)
    else:
        loop(below.span, lambda x: raise_(x, coarse[x + 1]))
    for repeat in range(SWEEPS):
        sweep(level, src, dst, scaled)
        src, dst = dst, src
    return src


def make_levels(refs):
    levels = []
    tools = refs[:6]
    refs = refs[6:]
    for depth in range(3):
        level = Level()
        level.step = (1, 1, 2)[depth]
        level.tools = tools if depth == 0 else None
        level.weight = 0.25**depth
        level.rho, level.scale, level.unscale, level.coef, level.scaled, level.one, level.two = refs[7 * depth : 7 * depth + 7]
        level.span = level.scale.shape[0]
        levels.append(level)
    return levels


def level_scratch(whole):
    span, rows, lanes = (whole[0] // 2, whole[1] // 2, whole[2] // 2)
    shapes = [
        pltpu.VMEM((2 * lanes, lanes), BF16),
        pltpu.VMEM((lanes, 2 * lanes), BF16),
        pltpu.VMEM((span * rows, 2 * lanes), F32),
        pltpu.VMEM((span * rows, lanes), F32),
        pltpu.VMEM((span, 2 * lanes // TILE, 2 * rows, TILE), F32),
        pltpu.VMEM((span, 2 * lanes // TILE, 2 * rows, TILE), F32),
    ]
    for depth in range(3):
        span = whole[0] // 2**depth
        plane = tuple(whole[1:]) if depth == 0 else (whole[1] // 2, whole[2] // 2)
        padded = pltpu.VMEM((span + 2,) + plane, F32)
        flat = pltpu.VMEM((span,) + plane, F32)
        shapes += [padded, flat, flat, pltpu.VMEM((6, span) + plane, F32), padded, padded, padded]
    return shapes


def clear_ends(ref):
    zero = jnp.zeros(ref.shape[1:], F32)
    ref[0] = zero
    ref[ref.shape[0] - 1] = zero


def prepare(levels, open_ref, density_ref, counts):
    span, rows, lanes = density_ref.shape[3:]
    for level in levels:
        for ref in (level.rho, level.scaled, level.one, level.two):
            clear_ends(ref)
    for i in range(counts[0]):
        for j in range(counts[1]):
            for k in range(counts[2]):
                levels[0].rho[
                    1 + span * i : 1 + span * (i + 1), rows * j : rows * (j + 1), lanes * k : lanes * (k + 1)
                ] = density_ref[i, k, j]
    for level, below in zip(levels[:-1], levels[1:]):

        def total(x, level=level):
            return level.rho[2 * x + 1] + level.rho[2 * x + 2]

        def store(x, mean, below=below):
            below.rho[x + 1] = mean

        if level.tools is not None:
            pair_matrices(level.tools)
            block_means(level.tools, below.span, total, store)
        else:
            loop(below.span, lambda x: store(x, pair_sum(total(x), level.step) * 0.125))
    for level in levels:
        build_level(level, open_ref)


def assemble(target, msg_ref, counts):
    planes, rows, lanes = msg_ref.shape[3:]
    span = planes - 3
    lane = iota((rows, lanes), 1)
    for i in range(counts[0]):
        for j in range(counts[1]):
            for k in range(counts[2]):
                at_rows = slice(rows * j, rows * (j + 1))
                at_lanes = slice(lanes * k, lanes * (k + 1))
                for x in range(span):
                    plane = msg_ref[i, k, j, x]
                    if x == 0 and i > 0:
                        plane = plane + msg_ref[i - 1, k, j, span]
                    if k > 0:
                        face = msg_ref[i, k - 1, j, span + 2]
                        face = ahead(face, x, 1) if x > 0 else face
                        plane = plane + jnp.where(lane == 0, face, 0.0)
                    target[1 + span * i + x, at_rows, at_lanes] = plane
                    if j > 0:
                        face = msg_ref[i, k, j - 1, span + 1, x : x + 1, :]
                        at_row = slice(rows * j, rows * j + 1)
                        target[1 + span * i + x, at_row, at_lanes] = (
                            target[1 + span * i + x, at_row, at_lanes] + face
                        )


def solve(levels, msg_ref, counts, kept):
    fine = levels[0]
    assemble(fine.scaled, msg_ref, counts)

    def scale(x):
        fine.scaled[x + 1] = fine.scaled[x + 1] * fine.scale[x]

    loop(fine.span, scale)
    first = cycle(levels, fine.scaled, fine.one, fine.two)

    def again(x):
        mid = first[x + 1]
        kept[x + 1] = mid
        fine.again[x + 1] = smoothed(fine, first, fine.scaled, x) - mid

    loop(fine.span, again)
    second = cycle(levels, fine.again, fine.one, fine.two)

    def add(x):
        kept[x + 1] = kept[x + 1] + second[x + 1]

    loop(fine.span, add)


def rises(kept, wide, slot, start, span):
    rows, lanes = kept.shape[1:]

    def body(x, unused):
        row = iota((rows, lanes), 0)
        lane = iota((rows, lanes), 1)
        mid = kept[start + x + 1]
        wide[slot, x] = kept[start + x + 2] - mid
        wide[slot + 1, x] = jnp.where(row == rows - 1, 0.0, ahead(mid, 1, 0)) - mid
        wide[slot + 2, x] = jnp.where(lane == lanes - 1, 0.0, ahead(mid, 1, 1)) - mid
        return unused

    lax.fori_loop(0, span, body, 0)


def own_block(wide, slot, rows, lanes):
    j = lax.axis_index("gy")
    k = lax.axis_index("gz")
    return wide[slot, :, pl.ds(pl.multiple_of(j * rows, rows), rows), pl.ds(pl.multiple_of(k * lanes, lanes), lanes)]


def project_kernel(counts, open_ref, density_ref, msg_ref, flux_ref, target_ref, new_ref, misfit_ref, out_ref, kept, extra, wide, *refs):
    levels = make_levels(refs)
    fine = levels[0]
    fine.again = extra
    clear_ends(kept)
    clear_ends(extra)
    prepare(levels, open_ref, density_ref, counts)
    solve(levels, msg_ref, counts, kept)
    _, span, rows, lanes = flux_ref.shape
    start = lax.axis_index("gx") * span
    rises(kept, wide, 0, start, span)

    def body(x, unused):
        ups = raw_upper(fine, open_ref, start + x)
        for d in range(3):
            wide[3 + d, x] = ups[d]
        return unused

    lax.fori_loop(0, span, body, 0)
    cells = counts[0] * counts[1] * counts[2] * span * rows * lanes
    fields = []
    for d in range(3):
        upper = own_block(wide, 3 + d, rows, lanes)
        fresh = flux_ref[d] - upper * own_block(wide, d, rows, lanes)
        new_ref[d] = fresh
        misfit = (fresh - target_ref[d]) / cells
        misfit_ref[d] = misfit
        fields.append(upper * misfit)
    write_message(out_ref, fields, 1.0)


def adjoint_kernel(counts, open_ref, density_ref, msg_ref, misfit_ref, cols_ref, win_ref, bias_ref, wout_ref, out_ref, upstream, kept, extra, wide, *refs):
    levels = make_levels(refs)
    fine = levels[0]
    fine.again = extra
    clear_ends(kept)
    clear_ends(extra)
    prepare(levels, open_ref, density_ref, counts)
    solve(levels, msg_ref, counts, kept)
    _, span, rows, lanes = misfit_ref.shape
    start = lax.axis_index("gx") * span
    rises(kept, wide, 0, start, span)
    first_end, second, third = local_outlets(open_ref, counts, (span, rows, lanes))
    chunk = rows * lanes
    upstream[...] = jnp.zeros(upstream.shape, F32)
    for d in range(3):
        block = misfit_ref[d] + own_block(wide, d, rows, lanes)
        for x in range(span):
            plane = block[x]
            if d == 0:
                plane = plane * first_end if x == span - 1 else plane
            else:
                plane = plane * (second if d == 1 else third)
            for y in range(rows):
                upstream[d : d + 1, x * chunk + y * lanes : x * chunk + (y + 1) * lanes] = plane[y : y + 1]
    across = (((1,), (1,)), ((), ()))
    feat, hidden_size = win_ref.shape
    grad_in = jnp.zeros((feat, hidden_size), F32)
    grad_out = jnp.zeros((8, hidden_size), F32)
    grad_bias = jnp.zeros((8, hidden_size), F32)
    ones = jnp.ones((8, chunk), BF16)
    for x in range(span):
        columns = cols_ref[:, x * chunk : (x + 1) * chunk]
        before = lax.dot_general(win_ref[...], columns, DOWN, preferred_element_type=F32) + bias_ref[...]
        gate = jax.nn.sigmoid(before)
        hidden = (before * gate).astype(BF16)
        up = upstream[:, x * chunk : (x + 1) * chunk].astype(BF16)
        grad_out = grad_out + lax.dot_general(up, hidden, across, preferred_element_type=F32)
        grad_hidden = jnp.dot(wout_ref[...], up[0:3], preferred_element_type=F32)
        grad_before = grad_hidden * (gate * (1.0 + before * (1.0 - gate)))
        high = grad_before.astype(BF16)
        low = (grad_before - high.astype(F32)).astype(BF16)
        grad_bias = grad_bias + lax.dot_general(ones, high, across, preferred_element_type=F32)
        grad_bias = grad_bias + lax.dot_general(ones, low, across, preferred_element_type=F32)
        grad_in = grad_in + lax.dot_general(columns, high, across, preferred_element_type=F32)
    out_ref[0:feat, :] = grad_in
    out_ref[feat : feat + 8, :] = grad_out
    out_ref[feat + 8 : feat + 16, :] = grad_bias


def gather_kernel(counts, total, block_ref, *refs):
    if total:
        out_ref, all_ref, keep_sem, send_sem, recv_sem = refs
    else:
        all_ref, keep_sem, send_sem, recv_sem = refs
    here = tuple(lax.axis_index(name) for name in AXES)

    def peer(axis, shift):
        where = list(here)
        where[axis] = lax.rem(here[axis] + shift, counts[axis])
        return tuple(where)

    barrier = pltpu.get_barrier_semaphore()
    for axis in range(3):
        for shift in range(1, counts[axis]):
            pl.semaphore_signal(barrier, inc=1, device_id=peer(axis, shift), device_id_type=pl.DeviceIdType.MESH)
    keep = pltpu.make_async_copy(block_ref, all_ref.at[here[0], here[2], here[1]], keep_sem)
    keep.start()
    pl.semaphore_wait(barrier, sum(counts) - 3)
    keep.wait()
    slot = 0
    for axis in (2, 0, 1):
        part = {
            2: all_ref.at[here[0], here[2], here[1]],
            0: all_ref.at[here[0], :, here[1]],
            1: all_ref.at[:, :, here[1]],
        }[axis]
        copies = []
        for shift in range(1, counts[axis]):
            copies.append(
                pltpu.make_async_remote_copy(
                    src_ref=part,
                    dst_ref=part,
                    send_sem=send_sem.at[slot],
                    recv_sem=recv_sem.at[slot],
                    device_id=peer(axis, shift),
                    device_id_type=pl.DeviceIdType.MESH,
                )
            )
            slot += 1
        for copy in copies:
            copy.start()
        for copy in copies:
            copy.wait()
    if total:
        result = jnp.zeros(out_ref.shape, F32)
        for i in range(counts[0]):
            for k in range(counts[2]):
                for j in range(counts[1]):
                    result = result + all_ref[i, k, j]
        out_ref[...] = result


def gather_blocks(block, counts, ident, total=False):
    vmem = pl.BlockSpec(memory_space=pltpu.VMEM)
    steps = sum(counts) - 3
    every = (counts[0], counts[2], counts[1]) + block.shape
    sems = [pltpu.SemaphoreType.DMA, pltpu.SemaphoreType.DMA((steps,)), pltpu.SemaphoreType.DMA((steps,))]
    held = [pltpu.VMEM(every, F32)] if total else []
    return pl.pallas_call(
        functools.partial(gather_kernel, counts, total),
        out_shape=jax.ShapeDtypeStruct(block.shape if total else every, F32),
        in_specs=[vmem],
        out_specs=vmem,
        scratch_shapes=held + sems,
        compiler_params=pltpu.CompilerParams(
            collective_id=ident, has_side_effects=True, vmem_limit_bytes=VMEM_BYTES
        ),
        name="gather_" + str(ident),
    )(block)


def whole_device(counts, velocity, features, density, target, weight_in, bias_in, weight_out, open_faces):
    shape = density.shape
    span, rows, lanes = shape
    whole = tuple(n * c for n, c in zip(shape, counts))
    feat, hidden_size = weight_in.shape
    cells = span * rows * lanes
    columns = features.reshape(feat, cells)
    bias = bias_in.reshape(hidden_size, 1)
    vmem = pl.BlockSpec(memory_space=pltpu.VMEM)
    smem = pl.BlockSpec(memory_space=pltpu.SMEM)
    params = pltpu.CompilerParams(vmem_limit_bytes=VMEM_BYTES)
    blocks = gather_blocks(density, counts, 1)
    field = jax.ShapeDtypeStruct((3,) + shape, F32)
    message = jax.ShapeDtypeStruct((span + 3, rows, lanes), F32)
    flux, msg = pl.pallas_call(
        functools.partial(forward_kernel, counts),
        out_shape=(field, message),
        in_specs=[smem] + [vmem] * 5,
        out_specs=(vmem, vmem),
        scratch_shapes=[pltpu.VMEM((3,) + shape, F32)],
        compiler_params=params,
        name="closure_forward",
    )(open_faces, columns, velocity, weight_in, bias, weight_out)
    sources = gather_blocks(msg, counts, 2)
    padded = pltpu.VMEM((whole[0] + 2,) + whole[1:], F32)
    wide = pltpu.VMEM((6, span) + whole[1:], F32)
    scratch = [padded, padded, wide] + level_scratch(whole)
    new_velocity, misfit, msg = pl.pallas_call(
        functools.partial(project_kernel, counts),
        out_shape=(field, field, message),
        in_specs=[smem] + [vmem] * 4,
        out_specs=(vmem, vmem, vmem),
        scratch_shapes=scratch,
        compiler_params=params,
        name="project",
    )(open_faces, blocks, sources, flux, target)
    sources = gather_blocks(msg, counts, 3)
    sums = pl.pallas_call(
        functools.partial(adjoint_kernel, counts),
        out_shape=jax.ShapeDtypeStruct((feat + 16, hidden_size), F32),
        in_specs=[smem] + [vmem] * 7,
        out_specs=vmem,
        scratch_shapes=[pltpu.VMEM((8, cells), F32)] + scratch,
        compiler_params=params,
        name="adjoint",
    )(open_faces, blocks, sources, misfit, columns, weight_in, bias, weight_out)
    sums = gather_blocks(sums, counts, 4, total=True)
    return new_velocity, sums[:feat], sums[feat + 8], sums[feat : feat + 3].T


def fits(mesh):
    return mesh.size <= 32


def solution(mesh):
    in_specs = (
        P(None, "gx", "gy", "gz"),
        P(None, "gx", "gy", "gz"),
        P("gx", "gy", "gz"),
        P(None, "gx", "gy", "gz"),
        P(),
        P(),
        P(),
        P(),
    )
    out_specs = (P(None, "gx", "gy", "gz"), P(), P(), P())
    counts = tuple(mesh.shape[name] for name in ("gx", "gy", "gz"))
    body = functools.partial(whole_device, counts) if fits(mesh) else per_device
    return jax.shard_map(
        body, mesh=mesh, in_specs=in_specs, out_specs=out_specs, check_vma=False
    )
```

```python
import functools

import jax
import jax.numpy as jnp
from jax import lax
from jax.experimental import pallas as pl
from jax.experimental.pallas import tpu as pltpu
from jax.sharding import PartitionSpec as P

SWEEPS = 3
COARSE_SWEEPS = 6


RELAXATION = 0.8
MASS_SHIFT = 0.05
SHAPES = ((-1, 1, 1), (1, -1, 1), (1, 1, -1))


def with_halo(shard, sides, width):
    for axis, dim in sides:
        count, length = (lax.axis_size(axis), shard.shape[dim])
        up = [(i, (i + 1) % count) for i in range(count - 1)]
        down = [(j, i) for i, j in up]
        last = lax.slice_in_dim(shard, length - width, length, axis=dim)
        leading = lax.slice_in_dim(shard, 0, width, axis=dim)
        before = lax.ppermute(last, axis, up)
        after = lax.ppermute(leading, axis, down)
        shard = jnp.concatenate([before, shard, after], axis=dim)
    return shard


def zero_padded(field):
    return jnp.pad(field, 1)


def halo_padded(field):
    return with_halo(field, (("gx", 0), ("gy", 1), ("gz", 2)), 1)


def deep_padded(field):
    return with_halo(field, (("gx", 0), ("gy", 1), ("gz", 2)), SWEEPS)


def deep_coefs(level_data):
    stacked = jnp.stack(list(level_data[1]) + list(level_data[2]) + [level_data[3]])
    extended = with_halo(stacked, (("gx", 1), ("gy", 2), ("gz", 3)), SWEEPS)
    diagonal = extended[6]
    safe_diagonal = jnp.where(diagonal > 0.0, diagonal, jnp.float32(1.0))
    return (
        (extended[0], extended[1], extended[2]),
        (extended[3], extended[4], extended[5]),
        diagonal,
        safe_diagonal,
    )


def trimmed(field, margin):
    span_first, span_second, span_third = field.shape
    return field[
        margin : span_first - margin, margin : span_second - margin, margin : span_third - margin
    ]


def apply_inner(iterate, extended, width):
    margin = SWEEPS - (width - 1)
    uppers = tuple((trimmed(extended[0][direction], margin) for direction in range(3)))
    lowers = tuple((trimmed(extended[1][direction], margin) for direction in range(3)))
    diagonal = trimmed(extended[2], margin)
    summed = neighbour_sum(iterate, uppers, lowers)
    return diagonal * iterate[1:-1, 1:-1, 1:-1] - summed


def sweep_inner(iterate, source_ext, extended, width):
    margin = SWEEPS - (width - 1)
    residue = trimmed(source_ext, margin) - apply_inner(iterate, extended, width)
    return iterate[1:-1, 1:-1, 1:-1] + RELAXATION * residue / trimmed(extended[3], margin)


def gather_whole(coarse_piece):
    span_first, span_second, span_third = coarse_piece.shape
    flattened = coarse_piece.reshape(1, span_first * span_second * span_third)
    gathered = lax.all_gather(flattened, ("gx", "gy", "gz"), axis=0, tiled=True)
    blocks = gathered.reshape(
        lax.axis_size("gx"),
        lax.axis_size("gy"),
        lax.axis_size("gz"),
        span_first,
        span_second,
        span_third,
    )
    return blocks.transpose(0, 3, 1, 4, 2, 5).reshape(
        lax.axis_size("gx") * span_first,
        lax.axis_size("gy") * span_second,
        lax.axis_size("gz") * span_third,
    )


def edge_factors(length, offset, whole_length, lower_flag, upper_flag):
    position = jnp.arange(length, dtype=jnp.int32) + offset
    lower = jnp.where(position == 0, lower_flag.astype(jnp.float32), jnp.float32(1.0))
    upper = jnp.where(
        position == whole_length - 1, upper_flag.astype(jnp.float32), jnp.float32(1.0)
    )
    return (lower, upper)


def coefficients(padded_density, factors, weight):
    centre = padded_density[1:-1, 1:-1, 1:-1]
    following = (
        padded_density[2:, 1:-1, 1:-1],
        padded_density[1:-1, 2:, 1:-1],
        padded_density[1:-1, 1:-1, 2:],
    )
    preceding = (
        padded_density[:-2, 1:-1, 1:-1],
        padded_density[1:-1, :-2, 1:-1],
        padded_density[1:-1, 1:-1, :-2],
    )
    upper_coefs = tuple(
        (
            weight
            * 2.0
            / (centre + following[direction])
            * factors[direction][1].reshape(SHAPES[direction])
            for direction in range(3)
        )
    )
    lower_coefs = tuple(
        (
            weight
            * 2.0
            / (centre + preceding[direction])
            * factors[direction][0].reshape(SHAPES[direction])
            for direction in range(3)
        )
    )
    diagonal = (
        MASS_SHIFT
        + upper_coefs[0]
        + lower_coefs[0]
        + upper_coefs[1]
        + lower_coefs[1]
        + upper_coefs[2]
        + lower_coefs[2]
    )
    return (upper_coefs, lower_coefs, diagonal)


def neighbour_sum(padded_field, upper_coefs, lower_coefs):
    summed = (
        upper_coefs[0] * padded_field[2:, 1:-1, 1:-1]
        + lower_coefs[0] * padded_field[:-2, 1:-1, 1:-1]
    )
    summed = (
        summed
        + upper_coefs[1] * padded_field[1:-1, 2:, 1:-1]
        + lower_coefs[1] * padded_field[1:-1, :-2, 1:-1]
    )
    summed = (
        summed
        + upper_coefs[2] * padded_field[1:-1, 1:-1, 2:]
        + lower_coefs[2] * padded_field[1:-1, 1:-1, :-2]
    )
    return summed


def apply_level(field, level_data):
    return level_data[3] * field - neighbour_sum(level_data[0](field), level_data[1], level_data[2])


def smooth_once(iterate, source, level_data):
    return iterate + RELAXATION * (source - apply_level(iterate, level_data)) / level_data[3]


def relax_from_zero(source, level_data, sweeps_count):
    iterate = RELAXATION * source / level_data[3]
    for repeat in range(sweeps_count - 1):
        iterate = smooth_once(iterate, source, level_data)
    return iterate


def restrict(field):
    span_first, span_second, span_third = field.shape
    return field.reshape(span_first // 2, 2, span_second // 2, 2, span_third // 2, 2).mean(
        axis=(1, 3, 5)
    )


def prolong(field):
    span_first, span_second, span_third = field.shape
    spread = jnp.broadcast_to(
        field[:, None, :, None, :, None], (span_first, 2, span_second, 2, span_third, 2)
    )
    return spread.reshape(2 * span_first, 2 * span_second, 2 * span_third)


def deep_cycle(source, extended_levels, coarse_solve):
    extended = extended_levels[0]
    source_ext = deep_padded(source)
    iterate = RELAXATION * source_ext / extended[3]
    width = SWEEPS
    for repeat in range(SWEEPS - 1):
        iterate = sweep_inner(iterate, source_ext, extended, width)
        width = width - 1
    margin = SWEEPS - (width - 1)
    residue = trimmed(source_ext, margin) - apply_inner(iterate, extended, width)
    iterate = trimmed(iterate, width)
    if len(extended_levels) > 1:
        correction = deep_cycle(restrict(residue), extended_levels[1:], coarse_solve)
    else:
        correction = coarse_solve(restrict(residue))
    iterate = deep_padded(iterate + prolong(correction))
    width = SWEEPS
    for repeat in range(SWEEPS):
        iterate = sweep_inner(iterate, source_ext, extended, width)
        width = width - 1
    return iterate


def deep_solve(source, levels, extended_levels, coarse_solve):
    iterate = deep_cycle(source, extended_levels, coarse_solve)
    iterate = iterate + deep_cycle(
        source - apply_level(iterate, levels[0]), extended_levels, coarse_solve
    )
    return iterate


def divergence(fluxes, padder):
    first = padder(fluxes[0])[:-2, 1:-1, 1:-1]
    second = padder(fluxes[1])[1:-1, :-2, 1:-1]
    third = padder(fluxes[2])[1:-1, 1:-1, :-2]
    return fluxes[0] - first + (fluxes[1] - second) + (fluxes[2] - third)


def upward_differences(field, padder):
    padded = padder(field)
    return (
        padded[2:, 1:-1, 1:-1] - field,
        padded[1:-1, 2:, 1:-1] - field,
        padded[1:-1, 1:-1, 2:] - field,
    )


def closure_plane(feature_plane, weight_in, bias_in, weight_out):
    columns = feature_plane.reshape(feature_plane.shape[0], -1)
    before = jnp.dot(weight_in.T, columns, preferred_element_type=jnp.float32) + bias_in[:, None]
    gate = jax.nn.sigmoid(before)
    hidden = (before * gate).astype(jnp.bfloat16)
    output = jnp.dot(weight_out.T, hidden, preferred_element_type=jnp.float32)
    return output.reshape((3,) + feature_plane.shape[1:])


def closure_field(features, weight_in, bias_in, weight_out):

    def one_plane(index):
        feature_plane = lax.dynamic_index_in_dim(features, index, 1, keepdims=False)
        return closure_plane(feature_plane, weight_in, bias_in, weight_out)

    stacked = lax.map(one_plane, jnp.arange(features.shape[1], dtype=jnp.int32))
    return jnp.moveaxis(stacked, 0, 1)


def gradient_plane(totals, feature_plane, grad_plane, weight_in, bias_in, weight_out):
    columns = feature_plane.reshape(feature_plane.shape[0], -1)
    before = jnp.dot(weight_in.T, columns, preferred_element_type=jnp.float32) + bias_in[:, None]
    gate = jax.nn.sigmoid(before)
    hidden = (before * gate).astype(jnp.bfloat16)
    upstream = grad_plane.reshape(3, -1).astype(jnp.bfloat16)
    grad_out = lax.dot_general(
        hidden, upstream, (((1,), (1,)), ((), ())), preferred_element_type=jnp.float32
    )
    grad_hidden = jnp.dot(weight_out, upstream, preferred_element_type=jnp.float32)
    grad_before = grad_hidden * (gate * (1.0 + before * (1.0 - gate)))
    grad_bias = jnp.sum(grad_before, axis=1)
    grad_in = lax.dot_general(
        columns,
        grad_before.astype(jnp.bfloat16),
        (((1,), (1,)), ((), ())),
        preferred_element_type=jnp.float32,
    )
    return (totals[0] + grad_in, totals[1] + grad_bias, totals[2] + grad_out)


def closure_gradients(features, grad_correction, weight_in, bias_in, weight_out):

    def step_plane(totals, index):
        feature_plane = lax.dynamic_index_in_dim(features, index, 1, keepdims=False)
        grad_plane = lax.dynamic_index_in_dim(grad_correction, index, 1, keepdims=False)
        return (
            gradient_plane(totals, feature_plane, grad_plane, weight_in, bias_in, weight_out),
            None,
        )

    start = (
        jnp.zeros(weight_in.shape, jnp.float32),
        jnp.zeros(bias_in.shape, jnp.float32),
        jnp.zeros(weight_out.shape, jnp.float32),
    )
    totals, unused = lax.scan(step_plane, start, jnp.arange(features.shape[1], dtype=jnp.int32))
    return totals


def training_step(
    velocity,
    features,
    target,
    weight_in,
    bias_in,
    weight_out,
    levels,
    solver,
    fine_factors,
    cells_total,
):
    padder = levels[0][0]
    upper_coefs = levels[0][1]
    outlets = tuple(
        (fine_factors[direction][1].reshape(SHAPES[direction]) for direction in range(3))
    )
    correction = closure_field(features, weight_in, bias_in, weight_out)
    fluxes = tuple(
        (
            (velocity[direction] + correction[direction]) * outlets[direction]
            for direction in range(3)
        )
    )
    source = -divergence(fluxes, padder)
    pressure = solver(source)
    rises = upward_differences(pressure, padder)
    new_velocity = jnp.stack(
        [fluxes[direction] - upper_coefs[direction] * rises[direction] for direction in range(3)]
    )
    misfit = (new_velocity - target) / cells_total
    weighted = tuple((upper_coefs[direction] * misfit[direction] for direction in range(3)))
    grad_pressure = divergence(weighted, padder)
    grad_source = solver(grad_pressure)
    drops = upward_differences(grad_source, padder)
    grad_correction = jnp.stack(
        [(misfit[direction] + drops[direction]) * outlets[direction] for direction in range(3)]
    )
    totals = closure_gradients(features, grad_correction, weight_in, bias_in, weight_out)
    return (new_velocity, totals)


def per_device(velocity, features, density, target, weight_in, bias_in, weight_out, open_faces):
    counts = (lax.axis_size("gx"), lax.axis_size("gy"), lax.axis_size("gz"))
    indices = (lax.axis_index("gx"), lax.axis_index("gy"), lax.axis_index("gz"))

    def level_factors(shape_now):
        return tuple(
            (
                edge_factors(
                    shape_now[direction],
                    indices[direction] * shape_now[direction],
                    shape_now[direction] * counts[direction],
                    open_faces[2 * direction],
                    open_faces[2 * direction + 1],
                )
                for direction in range(3)
            )
        )

    def make_level(level_density, weight):
        upper_coefs, lower_coefs, diagonal = coefficients(
            halo_padded(level_density), level_factors(level_density.shape), weight
        )
        return (halo_padded, upper_coefs, lower_coefs, diagonal)

    density_one = restrict(density)
    density_two = restrict(density_one)
    levels = (make_level(density, 1.0), make_level(density_one, 0.25))
    whole_density = gather_whole(density_two)
    whole_factors = tuple(
        (
            edge_factors(
                whole_density.shape[direction],
                0,
                whole_density.shape[direction],
                open_faces[2 * direction],
                open_faces[2 * direction + 1],
            )
            for direction in range(3)
        )
    )
    whole_upper, whole_lower, whole_diagonal = coefficients(
        zero_padded(whole_density), whole_factors, 0.0625
    )
    coarse_level = (zero_padded, whole_upper, whole_lower, whole_diagonal)

    def coarse_solve(source):
        whole_source = gather_whole(source)
        whole_iterate = relax_from_zero(whole_source, coarse_level, COARSE_SWEEPS)
        starts = tuple((indices[direction] * source.shape[direction] for direction in range(3)))
        return lax.dynamic_slice(whole_iterate, starts, source.shape)

    extended_levels = tuple((deep_coefs(level_data) for level_data in levels))

    def solver(source):
        return deep_solve(source, levels, extended_levels, coarse_solve)

    cells_total = density.size * counts[0] * counts[1] * counts[2]
    new_velocity, totals = training_step(
        velocity,
        features,
        target,
        weight_in,
        bias_in,
        weight_out,
        levels,
        solver,
        level_factors(density.shape),
        cells_total,
    )
    summed = lax.psum((totals[0], totals[1], totals[2]), ("gx", "gy", "gz"))
    return (new_velocity, summed[0], summed[1], summed[2])


F32 = jnp.float32
BF16 = jnp.bfloat16
MSG = 11
DOWN = (((0,), (0,)), ((), ()))
AXES = ("gx", "gy", "gz")
UNITS = (8, 128)
VMEM_BYTES = 56 * 1024 * 1024


def opened(open_ref, face):
    return open_ref[face].astype(F32)


def iota(shape, dim):
    return lax.broadcasted_iota(jnp.int32, shape, dim)


def ahead(plane, step, dim):
    return pltpu.roll(plane, plane.shape[dim] - step, dim)


def behind(plane, step, dim):
    return pltpu.roll(plane, step, dim)


def write_message(msg_ref, fields, sign):
    first, second, third = fields
    span, rows, lanes = first.shape
    row = iota((rows, lanes), 0)
    lane = iota((rows, lanes), 1)
    second_face = jnp.zeros((rows, lanes), F32)
    third_face = jnp.zeros((rows, lanes), F32)
    for x in range(span):
        total = first[x] + second[x] + third[x]
        if x > 0:
            total = total - first[x - 1]
        total = total - jnp.where(row == 0, 0.0, behind(second[x], 1, 0))
        total = total - jnp.where(lane == 0, 0.0, behind(third[x], 1, 1))
        msg_ref[x] = sign * total
        second_face = jnp.where(row == x, behind(second[x], x + 1, 0) if x < rows - 1 else second[x], second_face)
        third_face = jnp.where(lane == x, behind(third[x], x + 1, 1), third_face)
    msg_ref[span] = -sign * first[span - 1]
    msg_ref[span + 1] = -sign * second_face
    msg_ref[span + 2] = -sign * third_face


def local_outlets(open_ref, counts, shape):
    span, rows, lanes = shape
    here = [lax.axis_index(name) == count - 1 for name, count in zip(("gx", "gy", "gz"), counts)]
    one = jnp.float32(1.0)
    ends = [jnp.where(here[d], opened(open_ref, 2 * d + 1), one) for d in range(3)]
    row = iota((rows, lanes), 0)
    lane = iota((rows, lanes), 1)
    second = jnp.where(row == rows - 1, ends[1], one)
    third = jnp.where(lane == lanes - 1, ends[2], one)
    return ends[0], second, third


def forward_kernel(counts, open_ref, cols_ref, density_ref, vel_ref, win_ref, bias_ref, wout_ref, flux_ref, msg_ref, corr):
    _, span, rows, lanes = vel_ref.shape
    chunk = rows * lanes
    for x in range(span):
        before = lax.dot_general(win_ref[...], cols_ref[:, x * chunk : (x + 1) * chunk], DOWN, preferred_element_type=F32)
        before = before + bias_ref[...]
        hidden = (before * jax.nn.sigmoid(before)).astype(BF16)
        out = jnp.dot(wout_ref[...], hidden, preferred_element_type=F32)
        for d in range(3):
            for y in range(rows):
                corr[d, x, y : y + 1, :] = out[d : d + 1, y * lanes : (y + 1) * lanes]
    first_end, second, third = local_outlets(open_ref, counts, (span, rows, lanes))
    fields = []
    for d in range(3):
        planes = []
        for x in range(span):
            plane = vel_ref[d, x] + corr[d, x]
            if d == 0:
                plane = plane * first_end if x == span - 1 else plane
            else:
                plane = plane * (second if d == 1 else third)
            flux_ref[d, x] = plane
            planes.append(plane)
        fields.append(jnp.stack(planes))
    write_message(msg_ref, fields, -1.0)
    msg_ref[span + 3 : 2 * span + 3] = density_ref[...]


class Level:
    pass


def exact_dot(values, ones):
    high = values.astype(BF16)
    low = (values - high.astype(F32)).astype(BF16)
    total = jnp.dot(high, ones, preferred_element_type=F32)
    return total + jnp.dot(low, ones, preferred_element_type=F32)


def fold_matrices(tools):
    px, pz, flat = tools
    span, rows, lanes = flat.shape[0] - 2, flat.shape[1], flat.shape[2]
    row = iota(px.shape, 0)
    unit = lax.rem(row, span)
    source = (lax.rem(unit, UNITS[0]) * (span // UNITS[0]) + unit // UNITS[0]) * rows + row // span
    px[...] = jnp.where(source == iota(px.shape, 1), 1.0, 0.0).astype(BF16)
    column = iota(pz.shape, 1)
    source = lax.rem(column, UNITS[1]) * (lanes // UNITS[1]) + column // UNITS[1]
    pz[...] = jnp.where(source == iota(pz.shape, 0), 1.0, 0.0).astype(BF16)


def split_terms(values):
    high = values.astype(BF16)
    return high, (values - high.astype(F32)).astype(BF16)


def to_folded(tools, target):
    px, pz, flat = tools
    span, rows, lanes = flat.shape[0] - 2, flat.shape[1], flat.shape[2]
    values = exact_dot(flat[1 : span + 1].reshape(span * rows, lanes), pz[...])
    terms = [jnp.dot(px[...], term, preferred_element_type=F32) for term in split_terms(values)]
    target[1 : rows + 1] = (terms[0] + terms[1]).reshape(rows, span, lanes)


def from_folded(tools, source):
    px, pz, flat = tools
    span, rows, lanes = flat.shape[0] - 2, flat.shape[1], flat.shape[2]
    values = source[1 : rows + 1].reshape(rows * span, lanes)
    across = (((1,), (1,)), ((), ()))
    terms = [lax.dot_general(term, pz[...], across, preferred_element_type=F32) for term in split_terms(values)]
    values = terms[0] + terms[1]
    terms = [lax.dot_general(px[...], term, DOWN, preferred_element_type=F32) for term in split_terms(values)]
    flat[1 : span + 1] = (terms[0] + terms[1]).reshape(span, rows, lanes)


def part(plane, start, stop, dim):
    return plane[start:stop, :] if dim == 0 else plane[:, start:stop]


def join(parts, dim):
    return parts[0] if len(parts) == 1 else jnp.concatenate(parts, axis=dim)


def following(plane, dim):
    unit, size = UNITS[dim], plane.shape[dim]
    wrapped = pltpu.roll(part(plane, 0, unit, dim), unit - 1, dim)
    return join(([part(plane, unit, size, dim)] if size > unit else []) + [wrapped], dim)


def preceding(plane, dim):
    unit, size = UNITS[dim], plane.shape[dim]
    wrapped = pltpu.roll(part(plane, size - unit, size, dim), 1, dim)
    return join([wrapped] + ([part(plane, 0, size - unit, dim)] if size > unit else []), dim)


def pair_sum(plane):
    for dim in (0, 1):
        unit = UNITS[dim]
        count = plane.shape[dim] // unit
        pieces = [part(plane, n * unit, (n + 1) * unit, dim) for n in range(count)]
        plane = join([pieces[n] + pieces[n + 1] for n in range(0, count, 2)], dim)
    return plane


def spread(plane):
    for dim in (0, 1):
        unit = UNITS[dim]
        pieces = [part(plane, n * unit, (n + 1) * unit, dim) for n in range(plane.shape[dim] // unit)]
        plane = join([piece for piece in pieces for twice in range(2)], dim)
    return plane


def raw_upper(flat_rho, open_ref, x):
    rows, lanes = flat_rho.shape[1:]
    row = iota((rows, lanes), 0)
    lane = iota((rows, lanes), 1)
    step = 1
    rho = flat_rho[x + 1]
    last_row = row >= rows - step
    last_lane = lane >= lanes - step
    one = jnp.float32(1.0)
    up0 = jnp.where(x == flat_rho.shape[0] - 3, opened(open_ref, 1), one) * (2.0) / (rho + flat_rho[x + 2])
    up1 = (2.0) / (rho + jnp.where(last_row, 0.0, ahead(rho, step, 0)))
    up1 = up1 * jnp.where(last_row, opened(open_ref, 3), one)
    up2 = (2.0) / (rho + jnp.where(last_lane, 0.0, ahead(rho, step, 1)))
    up2 = up2 * jnp.where(last_lane, opened(open_ref, 5), one)
    return up0, up1, up2


def build_level(level, open_ref):
    rows, lanes = level.rho.shape[1:]

    def body(x, unused):
        row = iota((rows, lanes), 0)
        lane = iota((rows, lanes), 1)
        one = jnp.float32(1.0)
        twice = 2.0 * level.weight
        rho = level.rho[x + 1]
        last_row, first_row = row == rows - 1, row == 0
        last_lane, first_lane = lane == lanes - 1, lane == 0
        up1 = jnp.where(x == level.span - 1, opened(open_ref, 3), one) * twice / (rho + level.rho[x + 2])
        down1 = jnp.where(x == 0, opened(open_ref, 2), one) * twice / (rho + level.rho[x])
        up0 = twice / (rho + jnp.where(last_row, 0.0, following(rho, 0)))
        up2 = twice / (rho + jnp.where(last_lane, 0.0, following(rho, 1)))
        down0 = jnp.where(first_row, opened(open_ref, 0) * twice / rho, preceding(up0, 0))
        down2 = jnp.where(first_lane, opened(open_ref, 4) * twice / rho, preceding(up2, 1))
        up0 = up0 * jnp.where(last_row, opened(open_ref, 1), one)
        up2 = up2 * jnp.where(last_lane, opened(open_ref, 5), one)
        diagonal = MASS_SHIFT + up0 + down0 + up1 + down1 + up2 + down2
        scale = RELAXATION / diagonal
        level.scale[x] = scale
        level.unscale[x] = diagonal * (1.0 / RELAXATION)
        level.coef[0, x] = scale * up1
        level.coef[1, x] = scale * down1
        level.coef[2, x] = jnp.where(last_row, 0.0, scale * up0)
        level.coef[3, x] = jnp.where(first_row, 0.0, scale * down0)
        level.coef[4, x] = jnp.where(last_lane, 0.0, scale * up2)
        level.coef[5, x] = jnp.where(first_lane, 0.0, scale * down2)
        return unused

    lax.fori_loop(0, level.span, body, 0)


def smoothed(level, src, scaled, x):
    mid = src[x + 1]
    total = scaled[x + 1] + (1.0 - RELAXATION) * mid
    total = total + (level.coef[0, x] * src[x + 2] + level.coef[1, x] * src[x])
    total = total + (level.coef[2, x] * following(mid, 0) + level.coef[3, x] * preceding(mid, 0))
    return total + (level.coef[4, x] * following(mid, 1) + level.coef[5, x] * preceding(mid, 1))


def loop(count, body):
    def step(x, unused):
        body(x)
        return unused

    lax.fori_loop(0, count, step, 0, unroll=2)


def sweep(level, src, dst, scaled):
    def body(x):
        dst[x + 1] = smoothed(level, src, scaled, x)

    loop(level.span, body)


def cycle(levels, scaled, one, two):
    level = levels[0]
    if len(levels) == 1:
        src, dst, spare = scaled, one, two
        for repeat in range(COARSE_SWEEPS - 1):
            sweep(level, src, dst, scaled)
            src, dst, spare = dst, spare, dst
        return src
    sweep(level, scaled, one, scaled)
    src, dst = one, two
    for repeat in range(SWEEPS - 2):
        sweep(level, src, dst, scaled)
        src, dst = dst, src
    below = levels[1]

    def lower(x):
        even = (smoothed(level, src, scaled, 2 * x) - src[2 * x + 1]) * level.unscale[2 * x]
        odd = (smoothed(level, src, scaled, 2 * x + 1) - src[2 * x + 2]) * level.unscale[2 * x + 1]
        return even + odd

    def store(x, mean):
        below.scaled[x + 1] = mean * below.scale[x]

    loop(below.span, lambda x: store(x, pair_sum(lower(x)) * 0.125))
    coarse = cycle(levels[1:], below.scaled, below.one, below.two)

    def raise_(x, extra):
        src[2 * x + 1] = src[2 * x + 1] + extra
        src[2 * x + 2] = src[2 * x + 2] + extra

    loop(below.span, lambda x: raise_(x, spread(coarse[x + 1])))
    for repeat in range(SWEEPS):
        sweep(level, src, dst, scaled)
        src, dst = dst, src
    return src


def make_levels(refs):
    levels = []
    tools = refs[:3]
    refs = refs[3:]
    for depth in range(3):
        level = Level()
        level.tools = tools
        level.weight = 0.25**depth
        level.rho, level.scale, level.unscale, level.coef, level.scaled, level.one, level.two = refs[7 * depth : 7 * depth + 7]
        level.span = level.scale.shape[0]
        levels.append(level)
    return levels


def level_scratch(whole):
    shapes = [
        pltpu.VMEM((whole[0] * whole[1],) * 2, BF16),
        pltpu.VMEM((whole[2],) * 2, BF16),
        pltpu.VMEM((whole[0] + 2,) + whole[1:], F32),
    ]
    for depth in range(3):
        span = whole[1] // 2**depth
        plane = (whole[0] // 2**depth, whole[2] // 2**depth)
        padded = pltpu.VMEM((span + 2,) + plane, F32)
        flat = pltpu.VMEM((span,) + plane, F32)
        shapes += [padded, flat, flat, pltpu.VMEM((6, span) + plane, F32), padded, padded, padded]
    return shapes


def clear_ends(ref):
    zero = jnp.zeros(ref.shape[1:], F32)
    ref[0] = zero
    ref[ref.shape[0] - 1] = zero


def prepare(levels, open_ref, density_ref, counts, flat_rho):
    span = (density_ref.shape[3] - 3) // 2
    rows, lanes = density_ref.shape[4:]
    flat = levels[0].tools[2]
    clear_ends(flat_rho)
    clear_ends(flat)
    fold_matrices(levels[0].tools)
    for level in levels:
        for ref in (level.rho, level.scaled, level.one, level.two):
            clear_ends(ref)
    for i in range(counts[0]):
        for j in range(counts[1]):
            for k in range(counts[2]):
                flat_rho[
                    1 + span * i : 1 + span * (i + 1), rows * j : rows * (j + 1), lanes * k : lanes * (k + 1)
                ] = density_ref[i, k, j, span + 3 : 2 * span + 3]
    flat[...] = flat_rho[...]
    to_folded(levels[0].tools, levels[0].rho)
    for level, below in zip(levels[:-1], levels[1:]):

        def total(x, level=level):
            return level.rho[2 * x + 1] + level.rho[2 * x + 2]

        def store(x, mean, below=below):
            below.rho[x + 1] = mean

        loop(below.span, lambda x, total=total, store=store: store(x, pair_sum(total(x)) * 0.125))
    for level in levels:
        build_level(level, open_ref)


def assemble(target, msg_ref, counts):
    rows, lanes = msg_ref.shape[4:]
    span = (target.shape[0] - 2) // counts[0]
    lane = iota((rows, lanes), 1)
    for i in range(counts[0]):
        for j in range(counts[1]):
            for k in range(counts[2]):
                at_rows = slice(rows * j, rows * (j + 1))
                at_lanes = slice(lanes * k, lanes * (k + 1))
                for x in range(span):
                    plane = msg_ref[i, k, j, x]
                    if x == 0 and i > 0:
                        plane = plane + msg_ref[i - 1, k, j, span]
                    if k > 0:
                        face = msg_ref[i, k - 1, j, span + 2]
                        face = ahead(face, x, 1) if x > 0 else face
                        plane = plane + jnp.where(lane == 0, face, 0.0)
                    target[1 + span * i + x, at_rows, at_lanes] = plane
                    if j > 0:
                        face = msg_ref[i, k, j - 1, span + 1, x : x + 1, :]
                        at_row = slice(rows * j, rows * j + 1)
                        target[1 + span * i + x, at_row, at_lanes] = (
                            target[1 + span * i + x, at_row, at_lanes] + face
                        )


def solve(levels, msg_ref, counts, kept):
    fine = levels[0]
    flat = fine.tools[2]
    assemble(flat, msg_ref, counts)
    to_folded(fine.tools, fine.scaled)

    def scale(x):
        fine.scaled[x + 1] = fine.scaled[x + 1] * fine.scale[x]

    loop(fine.span, scale)
    first = cycle(levels, fine.scaled, fine.one, fine.two)

    def again(x):
        mid = first[x + 1]
        kept[x + 1] = mid
        fine.again[x + 1] = smoothed(fine, first, fine.scaled, x) - mid

    loop(fine.span, again)
    second = cycle(levels, fine.again, fine.one, fine.two)

    def add(x):
        kept[x + 1] = kept[x + 1] + second[x + 1]

    loop(fine.span, add)
    from_folded(fine.tools, kept)
    return flat


def rises(kept, wide, slot, start, span):
    rows, lanes = kept.shape[1:]

    def body(x, unused):
        row = iota((rows, lanes), 0)
        lane = iota((rows, lanes), 1)
        mid = kept[start + x + 1]
        wide[slot, x] = kept[start + x + 2] - mid
        wide[slot + 1, x] = jnp.where(row == rows - 1, 0.0, ahead(mid, 1, 0)) - mid
        wide[slot + 2, x] = jnp.where(lane == lanes - 1, 0.0, ahead(mid, 1, 1)) - mid
        return unused

    lax.fori_loop(0, span, body, 0)


def own_block(wide, slot, rows, lanes):
    j = lax.axis_index("gy")
    k = lax.axis_index("gz")
    return wide[slot, :, pl.ds(pl.multiple_of(j * rows, rows), rows), pl.ds(pl.multiple_of(k * lanes, lanes), lanes)]


def project_kernel(counts, open_ref, density_ref, flux_ref, target_ref, new_ref, misfit_ref, out_ref, kept, extra, flat_rho, wide, *refs):
    levels = make_levels(refs)
    fine = levels[0]
    fine.again = extra
    clear_ends(kept)
    clear_ends(extra)
    prepare(levels, open_ref, density_ref, counts, flat_rho)
    flat = solve(levels, density_ref, counts, kept)
    _, span, rows, lanes = flux_ref.shape
    start = lax.axis_index("gx") * span
    rises(flat, wide, 0, start, span)

    def body(x, unused):
        ups = raw_upper(flat_rho, open_ref, start + x)
        for d in range(3):
            wide[3 + d, x] = ups[d]
        return unused

    lax.fori_loop(0, span, body, 0)
    cells = counts[0] * counts[1] * counts[2] * span * rows * lanes
    fields = []
    for d in range(3):
        upper = own_block(wide, 3 + d, rows, lanes)
        fresh = flux_ref[d] - upper * own_block(wide, d, rows, lanes)
        new_ref[d] = fresh
        misfit = (fresh - target_ref[d]) / cells
        misfit_ref[d] = misfit
        fields.append(upper * misfit)
    write_message(out_ref, fields, 1.0)


def adjoint_kernel(counts, open_ref, density_ref, msg_ref, misfit_ref, cols_ref, win_ref, bias_ref, wout_ref, out_ref, upstream, kept, extra, flat_rho, wide, *refs):
    levels = make_levels(refs)
    fine = levels[0]
    fine.again = extra
    clear_ends(kept)
    clear_ends(extra)
    prepare(levels, open_ref, density_ref, counts, flat_rho)
    flat = solve(levels, msg_ref, counts, kept)
    _, span, rows, lanes = misfit_ref.shape
    start = lax.axis_index("gx") * span
    rises(flat, wide, 0, start, span)
    first_end, second, third = local_outlets(open_ref, counts, (span, rows, lanes))
    chunk = rows * lanes
    upstream[...] = jnp.zeros(upstream.shape, F32)
    for d in range(3):
        block = misfit_ref[d] + own_block(wide, d, rows, lanes)
        for x in range(span):
            plane = block[x]
            if d == 0:
                plane = plane * first_end if x == span - 1 else plane
            else:
                plane = plane * (second if d == 1 else third)
            for y in range(rows):
                upstream[d : d + 1, x * chunk + y * lanes : x * chunk + (y + 1) * lanes] = plane[y : y + 1]
    across = (((1,), (1,)), ((), ()))
    feat, hidden_size = win_ref.shape
    grad_in = jnp.zeros((feat, hidden_size), F32)
    grad_out = jnp.zeros((8, hidden_size), F32)
    grad_bias = jnp.zeros((8, hidden_size), F32)
    ones = jnp.ones((8, chunk), BF16)
    for x in range(span):
        columns = cols_ref[:, x * chunk : (x + 1) * chunk]
        before = lax.dot_general(win_ref[...], columns, DOWN, preferred_element_type=F32) + bias_ref[...]
        gate = jax.nn.sigmoid(before)
        hidden = (before * gate).astype(BF16)
        up = upstream[:, x * chunk : (x + 1) * chunk].astype(BF16)
        grad_out = grad_out + lax.dot_general(up, hidden, across, preferred_element_type=F32)
        grad_hidden = lax.dot_general(wout_ref[...], up[0:3], DOWN, preferred_element_type=F32)
        grad_before = grad_hidden * (gate * (1.0 + before * (1.0 - gate)))
        high = grad_before.astype(BF16)
        low = (grad_before - high.astype(F32)).astype(BF16)
        grad_bias = grad_bias + lax.dot_general(ones, high, across, preferred_element_type=F32)
        grad_bias = grad_bias + lax.dot_general(ones, low, across, preferred_element_type=F32)
        grad_in = grad_in + lax.dot_general(columns, high, across, preferred_element_type=F32)
    out_ref[0:feat, :] = grad_in
    out_ref[feat : feat + 8, :] = grad_out
    out_ref[feat + 8 : feat + 16, :] = grad_bias


def gather_kernel(counts, total, block_ref, *refs):
    if total:
        out_ref, all_ref, keep_sem, send_sem, recv_sem = refs
    else:
        all_ref, keep_sem, send_sem, recv_sem = refs
    here = tuple(lax.axis_index(name) for name in AXES)

    def peer(axis, shift):
        where = list(here)
        where[axis] = lax.rem(here[axis] + shift, counts[axis])
        return tuple(where)

    barrier = pltpu.get_barrier_semaphore()
    for axis in range(3):
        for shift in range(1, counts[axis]):
            pl.semaphore_signal(barrier, inc=1, device_id=peer(axis, shift), device_id_type=pl.DeviceIdType.MESH)
    keep = pltpu.make_async_copy(block_ref, all_ref.at[here[0], here[2], here[1]], keep_sem)
    keep.start()
    pl.semaphore_wait(barrier, sum(counts) - 3)
    keep.wait()
    slot = 0
    for axis in (2, 0, 1):
        part = {
            2: all_ref.at[here[0], here[2], here[1]],
            0: all_ref.at[here[0], :, here[1]],
            1: all_ref.at[:, :, here[1]],
        }[axis]
        copies = []
        for shift in range(1, counts[axis]):
            copies.append(
                pltpu.make_async_remote_copy(
                    src_ref=part,
                    dst_ref=part,
                    send_sem=send_sem.at[slot],
                    recv_sem=recv_sem.at[slot],
                    device_id=peer(axis, shift),
                    device_id_type=pl.DeviceIdType.MESH,
                )
            )
            slot += 1
        for copy in copies:
            copy.start()
        for copy in copies:
            copy.wait()
    if total:
        result = jnp.zeros(out_ref.shape, F32)
        for i in range(counts[0]):
            for k in range(counts[2]):
                for j in range(counts[1]):
                    result = result + all_ref[i, k, j]
        out_ref[...] = result


def gather_blocks(block, counts, ident, total=False):
    vmem = pl.BlockSpec(memory_space=pltpu.VMEM)
    steps = sum(counts) - 3
    every = (counts[0], counts[2], counts[1]) + block.shape
    sems = [pltpu.SemaphoreType.DMA, pltpu.SemaphoreType.DMA((steps,)), pltpu.SemaphoreType.DMA((steps,))]
    held = [pltpu.VMEM(every, F32)] if total else []
    return pl.pallas_call(
        functools.partial(gather_kernel, counts, total),
        out_shape=jax.ShapeDtypeStruct(block.shape if total else every, F32),
        in_specs=[vmem],
        out_specs=vmem,
        scratch_shapes=held + sems,
        compiler_params=pltpu.CompilerParams(
            collective_id=ident, has_side_effects=True, vmem_limit_bytes=VMEM_BYTES
        ),
        name="gather_" + str(ident),
    )(block)


def whole_device(counts, velocity, features, density, target, weight_in, bias_in, weight_out, open_faces):
    shape = density.shape
    span, rows, lanes = shape
    whole = tuple(n * c for n, c in zip(shape, counts))
    feat, hidden_size = weight_in.shape
    cells = span * rows * lanes
    columns = features.reshape(feat, cells)
    bias = bias_in.reshape(hidden_size, 1)
    vmem = pl.BlockSpec(memory_space=pltpu.VMEM)
    smem = pl.BlockSpec(memory_space=pltpu.SMEM)
    params = pltpu.CompilerParams(vmem_limit_bytes=VMEM_BYTES)
    field = jax.ShapeDtypeStruct((3,) + shape, F32)
    message = jax.ShapeDtypeStruct((span + 3, rows, lanes), F32)
    flux, msg = pl.pallas_call(
        functools.partial(forward_kernel, counts),
        out_shape=(field, jax.ShapeDtypeStruct((2 * span + 3, rows, lanes), F32)),
        in_specs=[smem] + [vmem] * 6,
        out_specs=(vmem, vmem),
        scratch_shapes=[pltpu.VMEM((3,) + shape, F32)],
        compiler_params=params,
        name="closure_forward",
    )(open_faces, columns, density, velocity, weight_in, bias, weight_out.T)
    blocks = gather_blocks(msg, counts, 1)
    padded = pltpu.VMEM((whole[0] + 2,) + whole[1:], F32)
    wide = pltpu.VMEM((6, span) + whole[1:], F32)
    folded = pltpu.VMEM((whole[1] + 2, whole[0], whole[2]), F32)
    scratch = [folded, folded, padded, wide] + level_scratch(whole)
    new_velocity, misfit, msg = pl.pallas_call(
        functools.partial(project_kernel, counts),
        out_shape=(field, field, message),
        in_specs=[smem] + [vmem] * 3,
        out_specs=(vmem, vmem, vmem),
        scratch_shapes=scratch,
        compiler_params=params,
        name="project",
    )(open_faces, blocks, flux, target)
    sources = gather_blocks(msg, counts, 2)
    sums = pl.pallas_call(
        functools.partial(adjoint_kernel, counts),
        out_shape=jax.ShapeDtypeStruct((feat + 16, hidden_size), F32),
        in_specs=[smem] + [vmem] * 7,
        out_specs=vmem,
        scratch_shapes=[pltpu.VMEM((8, cells), F32)] + scratch,
        compiler_params=params,
        name="adjoint",
    )(open_faces, blocks, sources, misfit, columns, weight_in, bias, weight_out.T)
    sums = gather_blocks(sums, counts, 3, total=True)
    return new_velocity, sums[:feat], sums[feat + 8], sums[feat : feat + 3].T


def fits(mesh):
    return mesh.size <= 32


def solution(mesh):
    in_specs = (
        P(None, "gx", "gy", "gz"),
        P(None, "gx", "gy", "gz"),
        P("gx", "gy", "gz"),
        P(None, "gx", "gy", "gz"),
        P(),
        P(),
        P(),
        P(),
    )
    out_specs = (P(None, "gx", "gy", "gz"), P(), P(), P())
    counts = tuple(mesh.shape[name] for name in ("gx", "gy", "gz"))
    body = functools.partial(whole_device, counts) if fits(mesh) else per_device
    return jax.shard_map(
        body, mesh=mesh, in_specs=in_specs, out_specs=out_specs, check_vma=False
    )
```

```python
import functools

import jax
import jax.numpy as jnp
from jax import lax
from jax.experimental import pallas as pl
from jax.experimental.pallas import tpu as pltpu
from jax.sharding import PartitionSpec as P

SWEEPS = 3
COARSE_SWEEPS = 6


RELAXATION = 0.8
MASS_SHIFT = 0.05
SHAPES = ((-1, 1, 1), (1, -1, 1), (1, 1, -1))


def with_halo(shard, sides, width):
    for axis, dim in sides:
        count, length = (lax.axis_size(axis), shard.shape[dim])
        up = [(i, (i + 1) % count) for i in range(count - 1)]
        down = [(j, i) for i, j in up]
        last = lax.slice_in_dim(shard, length - width, length, axis=dim)
        leading = lax.slice_in_dim(shard, 0, width, axis=dim)
        before = lax.ppermute(last, axis, up)
        after = lax.ppermute(leading, axis, down)
        shard = jnp.concatenate([before, shard, after], axis=dim)
    return shard


def zero_padded(field):
    return jnp.pad(field, 1)


def halo_padded(field):
    return with_halo(field, (("gx", 0), ("gy", 1), ("gz", 2)), 1)


def deep_padded(field):
    return with_halo(field, (("gx", 0), ("gy", 1), ("gz", 2)), SWEEPS)


def deep_coefs(level_data):
    stacked = jnp.stack(list(level_data[1]) + list(level_data[2]) + [level_data[3]])
    extended = with_halo(stacked, (("gx", 1), ("gy", 2), ("gz", 3)), SWEEPS)
    diagonal = extended[6]
    safe_diagonal = jnp.where(diagonal > 0.0, diagonal, jnp.float32(1.0))
    return (
        (extended[0], extended[1], extended[2]),
        (extended[3], extended[4], extended[5]),
        diagonal,
        safe_diagonal,
    )


def trimmed(field, margin):
    span_first, span_second, span_third = field.shape
    return field[
        margin : span_first - margin, margin : span_second - margin, margin : span_third - margin
    ]


def apply_inner(iterate, extended, width):
    margin = SWEEPS - (width - 1)
    uppers = tuple((trimmed(extended[0][direction], margin) for direction in range(3)))
    lowers = tuple((trimmed(extended[1][direction], margin) for direction in range(3)))
    diagonal = trimmed(extended[2], margin)
    summed = neighbour_sum(iterate, uppers, lowers)
    return diagonal * iterate[1:-1, 1:-1, 1:-1] - summed


def sweep_inner(iterate, source_ext, extended, width):
    margin = SWEEPS - (width - 1)
    residue = trimmed(source_ext, margin) - apply_inner(iterate, extended, width)
    return iterate[1:-1, 1:-1, 1:-1] + RELAXATION * residue / trimmed(extended[3], margin)


def gather_whole(coarse_piece):
    span_first, span_second, span_third = coarse_piece.shape
    flattened = coarse_piece.reshape(1, span_first * span_second * span_third)
    gathered = lax.all_gather(flattened, ("gx", "gy", "gz"), axis=0, tiled=True)
    blocks = gathered.reshape(
        lax.axis_size("gx"),
        lax.axis_size("gy"),
        lax.axis_size("gz"),
        span_first,
        span_second,
        span_third,
    )
    return blocks.transpose(0, 3, 1, 4, 2, 5).reshape(
        lax.axis_size("gx") * span_first,
        lax.axis_size("gy") * span_second,
        lax.axis_size("gz") * span_third,
    )


def edge_factors(length, offset, whole_length, lower_flag, upper_flag):
    position = jnp.arange(length, dtype=jnp.int32) + offset
    lower = jnp.where(position == 0, lower_flag.astype(jnp.float32), jnp.float32(1.0))
    upper = jnp.where(
        position == whole_length - 1, upper_flag.astype(jnp.float32), jnp.float32(1.0)
    )
    return (lower, upper)


def coefficients(padded_density, factors, weight):
    centre = padded_density[1:-1, 1:-1, 1:-1]
    following = (
        padded_density[2:, 1:-1, 1:-1],
        padded_density[1:-1, 2:, 1:-1],
        padded_density[1:-1, 1:-1, 2:],
    )
    preceding = (
        padded_density[:-2, 1:-1, 1:-1],
        padded_density[1:-1, :-2, 1:-1],
        padded_density[1:-1, 1:-1, :-2],
    )
    upper_coefs = tuple(
        (
            weight
            * 2.0
            / (centre + following[direction])
            * factors[direction][1].reshape(SHAPES[direction])
            for direction in range(3)
        )
    )
    lower_coefs = tuple(
        (
            weight
            * 2.0
            / (centre + preceding[direction])
            * factors[direction][0].reshape(SHAPES[direction])
            for direction in range(3)
        )
    )
    diagonal = (
        MASS_SHIFT
        + upper_coefs[0]
        + lower_coefs[0]
        + upper_coefs[1]
        + lower_coefs[1]
        + upper_coefs[2]
        + lower_coefs[2]
    )
    return (upper_coefs, lower_coefs, diagonal)


def neighbour_sum(padded_field, upper_coefs, lower_coefs):
    summed = (
        upper_coefs[0] * padded_field[2:, 1:-1, 1:-1]
        + lower_coefs[0] * padded_field[:-2, 1:-1, 1:-1]
    )
    summed = (
        summed
        + upper_coefs[1] * padded_field[1:-1, 2:, 1:-1]
        + lower_coefs[1] * padded_field[1:-1, :-2, 1:-1]
    )
    summed = (
        summed
        + upper_coefs[2] * padded_field[1:-1, 1:-1, 2:]
        + lower_coefs[2] * padded_field[1:-1, 1:-1, :-2]
    )
    return summed


def apply_level(field, level_data):
    return level_data[3] * field - neighbour_sum(level_data[0](field), level_data[1], level_data[2])


def smooth_once(iterate, source, level_data):
    return iterate + RELAXATION * (source - apply_level(iterate, level_data)) / level_data[3]


def relax_from_zero(source, level_data, sweeps_count):
    iterate = RELAXATION * source / level_data[3]
    for repeat in range(sweeps_count - 1):
        iterate = smooth_once(iterate, source, level_data)
    return iterate


def restrict(field):
    span_first, span_second, span_third = field.shape
    return field.reshape(span_first // 2, 2, span_second // 2, 2, span_third // 2, 2).mean(
        axis=(1, 3, 5)
    )


def prolong(field):
    span_first, span_second, span_third = field.shape
    spread = jnp.broadcast_to(
        field[:, None, :, None, :, None], (span_first, 2, span_second, 2, span_third, 2)
    )
    return spread.reshape(2 * span_first, 2 * span_second, 2 * span_third)


def deep_cycle(source, extended_levels, coarse_solve):
    extended = extended_levels[0]
    source_ext = deep_padded(source)
    iterate = RELAXATION * source_ext / extended[3]
    width = SWEEPS
    for repeat in range(SWEEPS - 1):
        iterate = sweep_inner(iterate, source_ext, extended, width)
        width = width - 1
    margin = SWEEPS - (width - 1)
    residue = trimmed(source_ext, margin) - apply_inner(iterate, extended, width)
    iterate = trimmed(iterate, width)
    if len(extended_levels) > 1:
        correction = deep_cycle(restrict(residue), extended_levels[1:], coarse_solve)
    else:
        correction = coarse_solve(restrict(residue))
    iterate = deep_padded(iterate + prolong(correction))
    width = SWEEPS
    for repeat in range(SWEEPS):
        iterate = sweep_inner(iterate, source_ext, extended, width)
        width = width - 1
    return iterate


def deep_solve(source, levels, extended_levels, coarse_solve):
    iterate = deep_cycle(source, extended_levels, coarse_solve)
    iterate = iterate + deep_cycle(
        source - apply_level(iterate, levels[0]), extended_levels, coarse_solve
    )
    return iterate


def divergence(fluxes, padder):
    first = padder(fluxes[0])[:-2, 1:-1, 1:-1]
    second = padder(fluxes[1])[1:-1, :-2, 1:-1]
    third = padder(fluxes[2])[1:-1, 1:-1, :-2]
    return fluxes[0] - first + (fluxes[1] - second) + (fluxes[2] - third)


def upward_differences(field, padder):
    padded = padder(field)
    return (
        padded[2:, 1:-1, 1:-1] - field,
        padded[1:-1, 2:, 1:-1] - field,
        padded[1:-1, 1:-1, 2:] - field,
    )


def closure_plane(feature_plane, weight_in, bias_in, weight_out):
    columns = feature_plane.reshape(feature_plane.shape[0], -1)
    before = jnp.dot(weight_in.T, columns, preferred_element_type=jnp.float32) + bias_in[:, None]
    gate = jax.nn.sigmoid(before)
    hidden = (before * gate).astype(jnp.bfloat16)
    output = jnp.dot(weight_out.T, hidden, preferred_element_type=jnp.float32)
    return output.reshape((3,) + feature_plane.shape[1:])


def closure_field(features, weight_in, bias_in, weight_out):

    def one_plane(index):
        feature_plane = lax.dynamic_index_in_dim(features, index, 1, keepdims=False)
        return closure_plane(feature_plane, weight_in, bias_in, weight_out)

    stacked = lax.map(one_plane, jnp.arange(features.shape[1], dtype=jnp.int32))
    return jnp.moveaxis(stacked, 0, 1)


def gradient_plane(totals, feature_plane, grad_plane, weight_in, bias_in, weight_out):
    columns = feature_plane.reshape(feature_plane.shape[0], -1)
    before = jnp.dot(weight_in.T, columns, preferred_element_type=jnp.float32) + bias_in[:, None]
    gate = jax.nn.sigmoid(before)
    hidden = (before * gate).astype(jnp.bfloat16)
    upstream = grad_plane.reshape(3, -1).astype(jnp.bfloat16)
    grad_out = lax.dot_general(
        hidden, upstream, (((1,), (1,)), ((), ())), preferred_element_type=jnp.float32
    )
    grad_hidden = jnp.dot(weight_out, upstream, preferred_element_type=jnp.float32)
    grad_before = grad_hidden * (gate * (1.0 + before * (1.0 - gate)))
    grad_bias = jnp.sum(grad_before, axis=1)
    grad_in = lax.dot_general(
        columns,
        grad_before.astype(jnp.bfloat16),
        (((1,), (1,)), ((), ())),
        preferred_element_type=jnp.float32,
    )
    return (totals[0] + grad_in, totals[1] + grad_bias, totals[2] + grad_out)


def closure_gradients(features, grad_correction, weight_in, bias_in, weight_out):

    def step_plane(totals, index):
        feature_plane = lax.dynamic_index_in_dim(features, index, 1, keepdims=False)
        grad_plane = lax.dynamic_index_in_dim(grad_correction, index, 1, keepdims=False)
        return (
            gradient_plane(totals, feature_plane, grad_plane, weight_in, bias_in, weight_out),
            None,
        )

    start = (
        jnp.zeros(weight_in.shape, jnp.float32),
        jnp.zeros(bias_in.shape, jnp.float32),
        jnp.zeros(weight_out.shape, jnp.float32),
    )
    totals, unused = lax.scan(step_plane, start, jnp.arange(features.shape[1], dtype=jnp.int32))
    return totals


def training_step(
    velocity,
    features,
    target,
    weight_in,
    bias_in,
    weight_out,
    levels,
    solver,
    fine_factors,
    cells_total,
):
    padder = levels[0][0]
    upper_coefs = levels[0][1]
    outlets = tuple(
        (fine_factors[direction][1].reshape(SHAPES[direction]) for direction in range(3))
    )
    correction = closure_field(features, weight_in, bias_in, weight_out)
    fluxes = tuple(
        (
            (velocity[direction] + correction[direction]) * outlets[direction]
            for direction in range(3)
        )
    )
    source = -divergence(fluxes, padder)
    pressure = solver(source)
    rises = upward_differences(pressure, padder)
    new_velocity = jnp.stack(
        [fluxes[direction] - upper_coefs[direction] * rises[direction] for direction in range(3)]
    )
    misfit = (new_velocity - target) / cells_total
    weighted = tuple((upper_coefs[direction] * misfit[direction] for direction in range(3)))
    grad_pressure = divergence(weighted, padder)
    grad_source = solver(grad_pressure)
    drops = upward_differences(grad_source, padder)
    grad_correction = jnp.stack(
        [(misfit[direction] + drops[direction]) * outlets[direction] for direction in range(3)]
    )
    totals = closure_gradients(features, grad_correction, weight_in, bias_in, weight_out)
    return (new_velocity, totals)


def per_device(velocity, features, density, target, weight_in, bias_in, weight_out, open_faces):
    counts = (lax.axis_size("gx"), lax.axis_size("gy"), lax.axis_size("gz"))
    indices = (lax.axis_index("gx"), lax.axis_index("gy"), lax.axis_index("gz"))

    def level_factors(shape_now):
        return tuple(
            (
                edge_factors(
                    shape_now[direction],
                    indices[direction] * shape_now[direction],
                    shape_now[direction] * counts[direction],
                    open_faces[2 * direction],
                    open_faces[2 * direction + 1],
                )
                for direction in range(3)
            )
        )

    def make_level(level_density, weight):
        upper_coefs, lower_coefs, diagonal = coefficients(
            halo_padded(level_density), level_factors(level_density.shape), weight
        )
        return (halo_padded, upper_coefs, lower_coefs, diagonal)

    density_one = restrict(density)
    density_two = restrict(density_one)
    levels = (make_level(density, 1.0), make_level(density_one, 0.25))
    whole_density = gather_whole(density_two)
    whole_factors = tuple(
        (
            edge_factors(
                whole_density.shape[direction],
                0,
                whole_density.shape[direction],
                open_faces[2 * direction],
                open_faces[2 * direction + 1],
            )
            for direction in range(3)
        )
    )
    whole_upper, whole_lower, whole_diagonal = coefficients(
        zero_padded(whole_density), whole_factors, 0.0625
    )
    coarse_level = (zero_padded, whole_upper, whole_lower, whole_diagonal)

    def coarse_solve(source):
        whole_source = gather_whole(source)
        whole_iterate = relax_from_zero(whole_source, coarse_level, COARSE_SWEEPS)
        starts = tuple((indices[direction] * source.shape[direction] for direction in range(3)))
        return lax.dynamic_slice(whole_iterate, starts, source.shape)

    extended_levels = tuple((deep_coefs(level_data) for level_data in levels))

    def solver(source):
        return deep_solve(source, levels, extended_levels, coarse_solve)

    cells_total = density.size * counts[0] * counts[1] * counts[2]
    new_velocity, totals = training_step(
        velocity,
        features,
        target,
        weight_in,
        bias_in,
        weight_out,
        levels,
        solver,
        level_factors(density.shape),
        cells_total,
    )
    summed = lax.psum((totals[0], totals[1], totals[2]), ("gx", "gy", "gz"))
    return (new_velocity, summed[0], summed[1], summed[2])


F32 = jnp.float32
BF16 = jnp.bfloat16
MSG = 11
DOWN = (((0,), (0,)), ((), ()))
AXES = ("gx", "gy", "gz")
UNITS = (8, 128)
VMEM_BYTES = 56 * 1024 * 1024


def opened(open_ref, face):
    return open_ref[face].astype(F32)


def iota(shape, dim):
    return lax.broadcasted_iota(jnp.int32, shape, dim)


def ahead(plane, step, dim):
    return pltpu.roll(plane, plane.shape[dim] - step, dim)


def behind(plane, step, dim):
    return pltpu.roll(plane, step, dim)


def write_message(msg_ref, fields, sign):
    first, second, third = fields
    span, rows, lanes = first.shape
    row = iota((rows, lanes), 0)
    lane = iota((rows, lanes), 1)
    second_face = jnp.zeros((rows, lanes), F32)
    third_face = jnp.zeros((rows, lanes), F32)
    for x in range(span):
        total = first[x] + second[x] + third[x]
        if x > 0:
            total = total - first[x - 1]
        total = total - jnp.where(row == 0, 0.0, behind(second[x], 1, 0))
        total = total - jnp.where(lane == 0, 0.0, behind(third[x], 1, 1))
        msg_ref[x] = sign * total
        second_face = jnp.where(row == x, behind(second[x], x + 1, 0) if x < rows - 1 else second[x], second_face)
        third_face = jnp.where(lane == x, behind(third[x], x + 1, 1), third_face)
    msg_ref[span] = -sign * first[span - 1]
    msg_ref[span + 1] = -sign * second_face
    msg_ref[span + 2] = -sign * third_face


def local_outlets(open_ref, counts, shape):
    span, rows, lanes = shape
    here = [lax.axis_index(name) == count - 1 for name, count in zip(("gx", "gy", "gz"), counts)]
    one = jnp.float32(1.0)
    ends = [jnp.where(here[d], opened(open_ref, 2 * d + 1), one) for d in range(3)]
    row = iota((rows, lanes), 0)
    lane = iota((rows, lanes), 1)
    second = jnp.where(row == rows - 1, ends[1], one)
    third = jnp.where(lane == lanes - 1, ends[2], one)
    return ends[0], second, third


def forward_kernel(counts, open_ref, cols_ref, density_ref, vel_ref, win_ref, bias_ref, wout_ref, flux_ref, msg_ref, corr):
    _, span, rows, lanes = vel_ref.shape
    chunk = rows * lanes
    for x in range(span):
        before = lax.dot_general(win_ref[...], cols_ref[:, x * chunk : (x + 1) * chunk], DOWN, preferred_element_type=F32)
        before = before + bias_ref[...]
        hidden = (before * jax.nn.sigmoid(before)).astype(BF16)
        out = jnp.dot(wout_ref[...], hidden, preferred_element_type=F32)
        for d in range(3):
            for y in range(rows):
                corr[d, x, y : y + 1, :] = out[d : d + 1, y * lanes : (y + 1) * lanes]
    first_end, second, third = local_outlets(open_ref, counts, (span, rows, lanes))
    fields = []
    for d in range(3):
        planes = []
        for x in range(span):
            plane = vel_ref[d, x] + corr[d, x]
            if d == 0:
                plane = plane * first_end if x == span - 1 else plane
            else:
                plane = plane * (second if d == 1 else third)
            flux_ref[d, x] = plane
            planes.append(plane)
        fields.append(jnp.stack(planes))
    write_message(msg_ref, fields, -1.0)
    msg_ref[span + 3 : 2 * span + 3] = density_ref[...]


class Level:
    pass


def exact_dot(values, ones):
    high = values.astype(BF16)
    low = (values - high.astype(F32)).astype(BF16)
    total = jnp.dot(high, ones, preferred_element_type=F32)
    return total + jnp.dot(low, ones, preferred_element_type=F32)


def fold_matrices(tools):
    px, pz, flat = tools
    span, rows, lanes = flat.shape[0] - 2, flat.shape[1], flat.shape[2]
    row = iota(px.shape, 0)
    unit = lax.rem(row, span)
    source = (lax.rem(unit, UNITS[0]) * (span // UNITS[0]) + unit // UNITS[0]) * rows + row // span
    px[...] = jnp.where(source == iota(px.shape, 1), 1.0, 0.0).astype(BF16)
    column = iota(pz.shape, 1)
    source = lax.rem(column, UNITS[1]) * (lanes // UNITS[1]) + column // UNITS[1]
    pz[...] = jnp.where(source == iota(pz.shape, 0), 1.0, 0.0).astype(BF16)


def split_terms(values):
    high = values.astype(BF16)
    return high, (values - high.astype(F32)).astype(BF16)


def to_folded(tools, target):
    px, pz, flat = tools
    span, rows, lanes = flat.shape[0] - 2, flat.shape[1], flat.shape[2]
    values = exact_dot(flat[1 : span + 1].reshape(span * rows, lanes), pz[...])
    terms = [jnp.dot(px[...], term, preferred_element_type=F32) for term in split_terms(values)]
    target[1 : rows + 1] = (terms[0] + terms[1]).reshape(rows, span, lanes)


def from_folded(tools, source):
    px, pz, flat = tools
    span, rows, lanes = flat.shape[0] - 2, flat.shape[1], flat.shape[2]
    values = source[1 : rows + 1].reshape(rows * span, lanes)
    across = (((1,), (1,)), ((), ()))
    terms = [lax.dot_general(term, pz[...], across, preferred_element_type=F32) for term in split_terms(values)]
    values = terms[0] + terms[1]
    terms = [lax.dot_general(px[...], term, DOWN, preferred_element_type=F32) for term in split_terms(values)]
    flat[1 : span + 1] = (terms[0] + terms[1]).reshape(span, rows, lanes)


def part(plane, start, stop, dim):
    return plane[start:stop, :] if dim == 0 else plane[:, start:stop]


def join(parts, dim):
    return parts[0] if len(parts) == 1 else jnp.concatenate(parts, axis=dim)


def following(plane, dim):
    unit, size = UNITS[dim], plane.shape[dim]
    wrapped = pltpu.roll(part(plane, 0, unit, dim), unit - 1, dim)
    return join(([part(plane, unit, size, dim)] if size > unit else []) + [wrapped], dim)


def preceding(plane, dim):
    unit, size = UNITS[dim], plane.shape[dim]
    wrapped = pltpu.roll(part(plane, size - unit, size, dim), 1, dim)
    return join([wrapped] + ([part(plane, 0, size - unit, dim)] if size > unit else []), dim)


def pair_sum(plane):
    for dim in (0, 1):
        unit = UNITS[dim]
        count = plane.shape[dim] // unit
        pieces = [part(plane, n * unit, (n + 1) * unit, dim) for n in range(count)]
        plane = join([pieces[n] + pieces[n + 1] for n in range(0, count, 2)], dim)
    return plane


def spread(plane):
    for dim in (0, 1):
        unit = UNITS[dim]
        pieces = [part(plane, n * unit, (n + 1) * unit, dim) for n in range(plane.shape[dim] // unit)]
        plane = join([piece for piece in pieces for twice in range(2)], dim)
    return plane


def raw_upper(flat_rho, open_ref, x):
    rows, lanes = flat_rho.shape[1:]
    row = iota((rows, lanes), 0)
    lane = iota((rows, lanes), 1)
    step = 1
    rho = flat_rho[x + 1]
    last_row = row >= rows - step
    last_lane = lane >= lanes - step
    one = jnp.float32(1.0)
    up0 = jnp.where(x == flat_rho.shape[0] - 3, opened(open_ref, 1), one) * (2.0) / (rho + flat_rho[x + 2])
    up1 = (2.0) / (rho + jnp.where(last_row, 0.0, ahead(rho, step, 0)))
    up1 = up1 * jnp.where(last_row, opened(open_ref, 3), one)
    up2 = (2.0) / (rho + jnp.where(last_lane, 0.0, ahead(rho, step, 1)))
    up2 = up2 * jnp.where(last_lane, opened(open_ref, 5), one)
    return up0, up1, up2


def build_level(level, open_ref):
    rows, lanes = level.rho.shape[1:]

    def body(x, unused):
        row = iota((rows, lanes), 0)
        lane = iota((rows, lanes), 1)
        one = jnp.float32(1.0)
        twice = 2.0 * level.weight
        rho = level.rho[x + 1]
        last_row, first_row = row == rows - 1, row == 0
        last_lane, first_lane = lane == lanes - 1, lane == 0
        up1 = jnp.where(x == level.span - 1, opened(open_ref, 3), one) * twice / (rho + level.rho[x + 2])
        down1 = jnp.where(x == 0, opened(open_ref, 2), one) * twice / (rho + level.rho[x])
        up0 = twice / (rho + jnp.where(last_row, 0.0, following(rho, 0)))
        up2 = twice / (rho + jnp.where(last_lane, 0.0, following(rho, 1)))
        down0 = jnp.where(first_row, opened(open_ref, 0) * twice / rho, preceding(up0, 0))
        down2 = jnp.where(first_lane, opened(open_ref, 4) * twice / rho, preceding(up2, 1))
        up0 = up0 * jnp.where(last_row, opened(open_ref, 1), one)
        up2 = up2 * jnp.where(last_lane, opened(open_ref, 5), one)
        diagonal = MASS_SHIFT + up0 + down0 + up1 + down1 + up2 + down2
        scale = RELAXATION / diagonal
        level.scale[x] = scale
        level.unscale[x] = diagonal * (1.0 / RELAXATION)
        level.coef[0, x] = scale * up1
        level.coef[1, x] = scale * down1
        level.coef[2, x] = jnp.where(last_row, 0.0, scale * up0)
        level.coef[3, x] = jnp.where(first_row, 0.0, scale * down0)
        level.coef[4, x] = jnp.where(last_lane, 0.0, scale * up2)
        level.coef[5, x] = jnp.where(first_lane, 0.0, scale * down2)
        return unused

    lax.fori_loop(0, level.span, body, 0)


def smoothed(level, src, scaled, x):
    mid = src[x + 1]
    total = scaled[x + 1] + (1.0 - RELAXATION) * mid
    total = total + (level.coef[0, x] * src[x + 2] + level.coef[1, x] * src[x])
    total = total + (level.coef[2, x] * following(mid, 0) + level.coef[3, x] * preceding(mid, 0))
    return total + (level.coef[4, x] * following(mid, 1) + level.coef[5, x] * preceding(mid, 1))


def loop(count, body):
    def step(x, unused):
        body(x)
        return unused

    lax.fori_loop(0, count, step, 0, unroll=2)


def sweep(level, src, dst, scaled):
    def body(x):
        dst[x + 1] = smoothed(level, src, scaled, x)

    loop(level.span, body)


def cycle(levels, scaled, one, two):
    level = levels[0]
    if len(levels) == 1:
        src, dst, spare = scaled, one, two
        for repeat in range(COARSE_SWEEPS - 1):
            sweep(level, src, dst, scaled)
            src, dst, spare = dst, spare, dst
        return src
    sweep(level, scaled, one, scaled)
    src, dst = one, two
    for repeat in range(SWEEPS - 2):
        sweep(level, src, dst, scaled)
        src, dst = dst, src
    below = levels[1]

    def lower(x):
        even = (smoothed(level, src, scaled, 2 * x) - src[2 * x + 1]) * level.unscale[2 * x]
        odd = (smoothed(level, src, scaled, 2 * x + 1) - src[2 * x + 2]) * level.unscale[2 * x + 1]
        return even + odd

    def store(x, mean):
        below.scaled[x + 1] = mean * below.scale[x]

    loop(below.span, lambda x: store(x, pair_sum(lower(x)) * 0.125))
    coarse = cycle(levels[1:], below.scaled, below.one, below.two)

    def raise_(x, extra):
        src[2 * x + 1] = src[2 * x + 1] + extra
        src[2 * x + 2] = src[2 * x + 2] + extra

    loop(below.span, lambda x: raise_(x, spread(coarse[x + 1])))
    for repeat in range(SWEEPS):
        sweep(level, src, dst, scaled)
        src, dst = dst, src
    return src


def make_levels(refs):
    levels = []
    tools = refs[:3]
    refs = refs[3:]
    for depth in range(3):
        level = Level()
        level.tools = tools
        level.weight = 0.25**depth
        level.rho, level.scale, level.unscale, level.coef, level.scaled, level.one, level.two = refs[7 * depth : 7 * depth + 7]
        level.span = level.scale.shape[0]
        levels.append(level)
    return levels


def level_scratch(whole):
    shapes = [
        pltpu.VMEM((whole[0] * whole[1],) * 2, BF16),
        pltpu.VMEM((whole[2],) * 2, BF16),
        pltpu.VMEM((whole[0] + 2,) + whole[1:], F32),
    ]
    for depth in range(3):
        span = whole[1] // 2**depth
        plane = (whole[0] // 2**depth, whole[2] // 2**depth)
        padded = pltpu.VMEM((span + 2,) + plane, F32)
        flat = pltpu.VMEM((span,) + plane, F32)
        shapes += [padded, flat, flat, pltpu.VMEM((6, span) + plane, F32), padded, padded, padded]
    return shapes


def clear_ends(ref):
    zero = jnp.zeros(ref.shape[1:], F32)
    ref[0] = zero
    ref[ref.shape[0] - 1] = zero


def prepare(levels, open_ref, density_ref, counts, flat_rho):
    span = (density_ref.shape[3] - 3) // 2
    rows, lanes = density_ref.shape[4:]
    flat = levels[0].tools[2]
    clear_ends(flat_rho)
    clear_ends(flat)
    fold_matrices(levels[0].tools)
    for level in levels:
        for ref in (level.rho, level.scaled, level.one, level.two):
            clear_ends(ref)
    for i in range(counts[0]):
        for j in range(counts[1]):
            for k in range(counts[2]):
                flat_rho[
                    1 + span * i : 1 + span * (i + 1), rows * j : rows * (j + 1), lanes * k : lanes * (k + 1)
                ] = density_ref[i, k, j, span + 3 : 2 * span + 3]
    flat[...] = flat_rho[...]
    to_folded(levels[0].tools, levels[0].rho)
    for level, below in zip(levels[:-1], levels[1:]):

        def total(x, level=level):
            return level.rho[2 * x + 1] + level.rho[2 * x + 2]

        def store(x, mean, below=below):
            below.rho[x + 1] = mean

        loop(below.span, lambda x, total=total, store=store: store(x, pair_sum(total(x)) * 0.125))
    for level in levels:
        build_level(level, open_ref)


def assemble(target, msg_ref, counts):
    rows, lanes = msg_ref.shape[4:]
    span = (target.shape[0] - 2) // counts[0]
    lane = iota((rows, lanes), 1)
    for i in range(counts[0]):
        for j in range(counts[1]):
            for k in range(counts[2]):
                at_rows = slice(rows * j, rows * (j + 1))
                at_lanes = slice(lanes * k, lanes * (k + 1))
                for x in range(span):
                    plane = msg_ref[i, k, j, x]
                    if x == 0 and i > 0:
                        plane = plane + msg_ref[i - 1, k, j, span]
                    if k > 0:
                        face = msg_ref[i, k - 1, j, span + 2]
                        face = ahead(face, x, 1) if x > 0 else face
                        plane = plane + jnp.where(lane == 0, face, 0.0)
                    target[1 + span * i + x, at_rows, at_lanes] = plane
                    if j > 0:
                        face = msg_ref[i, k, j - 1, span + 1, x : x + 1, :]
                        at_row = slice(rows * j, rows * j + 1)
                        target[1 + span * i + x, at_row, at_lanes] = (
                            target[1 + span * i + x, at_row, at_lanes] + face
                        )


def solve(levels, msg_ref, counts, kept):
    fine = levels[0]
    flat = fine.tools[2]
    assemble(flat, msg_ref, counts)
    to_folded(fine.tools, fine.scaled)

    def scale(x):
        fine.scaled[x + 1] = fine.scaled[x + 1] * fine.scale[x]

    loop(fine.span, scale)
    first = cycle(levels, fine.scaled, fine.one, fine.two)

    def again(x):
        mid = first[x + 1]
        kept[x + 1] = mid
        fine.again[x + 1] = smoothed(fine, first, fine.scaled, x) - mid

    loop(fine.span, again)
    second = cycle(levels, fine.again, fine.one, fine.two)

    def add(x):
        kept[x + 1] = kept[x + 1] + second[x + 1]

    loop(fine.span, add)
    from_folded(fine.tools, kept)
    return flat


def rises(kept, wide, slot, start, span):
    rows, lanes = kept.shape[1:]

    def body(x, unused):
        row = iota((rows, lanes), 0)
        lane = iota((rows, lanes), 1)
        mid = kept[start + x + 1]
        wide[slot, x] = kept[start + x + 2] - mid
        wide[slot + 1, x] = jnp.where(row == rows - 1, 0.0, ahead(mid, 1, 0)) - mid
        wide[slot + 2, x] = jnp.where(lane == lanes - 1, 0.0, ahead(mid, 1, 1)) - mid
        return unused

    lax.fori_loop(0, span, body, 0)


def own_block(wide, slot, rows, lanes):
    j = lax.axis_index("gy")
    k = lax.axis_index("gz")
    return wide[slot, :, pl.ds(pl.multiple_of(j * rows, rows), rows), pl.ds(pl.multiple_of(k * lanes, lanes), lanes)]


def project_kernel(counts, open_ref, density_ref, flux_ref, target_ref, new_ref, misfit_ref, out_ref, kept, extra, flat_rho, wide, *refs):
    levels = make_levels(refs)
    fine = levels[0]
    fine.again = extra
    clear_ends(kept)
    clear_ends(extra)
    prepare(levels, open_ref, density_ref, counts, flat_rho)
    flat = solve(levels, density_ref, counts, kept)
    _, span, rows, lanes = flux_ref.shape
    start = lax.axis_index("gx") * span
    rises(flat, wide, 0, start, span)

    def body(x, unused):
        ups = raw_upper(flat_rho, open_ref, start + x)
        for d in range(3):
            wide[3 + d, x] = ups[d]
        return unused

    lax.fori_loop(0, span, body, 0)
    cells = counts[0] * counts[1] * counts[2] * span * rows * lanes
    fields = []
    for d in range(3):
        upper = own_block(wide, 3 + d, rows, lanes)
        fresh = flux_ref[d] - upper * own_block(wide, d, rows, lanes)
        new_ref[d] = fresh
        misfit = (fresh - target_ref[d]) / cells
        misfit_ref[d] = misfit
        fields.append(upper * misfit)
    write_message(out_ref, fields, 1.0)


def adjoint_kernel(counts, open_ref, density_ref, msg_ref, misfit_ref, cols_ref, win_ref, bias_ref, wout_ref, out_ref, upstream, kept, extra, flat_rho, wide, *refs):
    levels = make_levels(refs)
    fine = levels[0]
    fine.again = extra
    clear_ends(kept)
    clear_ends(extra)
    prepare(levels, open_ref, density_ref, counts, flat_rho)
    flat = solve(levels, msg_ref, counts, kept)
    _, span, rows, lanes = misfit_ref.shape
    start = lax.axis_index("gx") * span
    rises(flat, wide, 0, start, span)
    first_end, second, third = local_outlets(open_ref, counts, (span, rows, lanes))
    chunk = rows * lanes
    upstream[...] = jnp.zeros(upstream.shape, F32)
    for d in range(3):
        block = misfit_ref[d] + own_block(wide, d, rows, lanes)
        for x in range(span):
            plane = block[x]
            if d == 0:
                plane = plane * first_end if x == span - 1 else plane
            else:
                plane = plane * (second if d == 1 else third)
            for y in range(rows):
                upstream[d : d + 1, x * chunk + y * lanes : x * chunk + (y + 1) * lanes] = plane[y : y + 1]
    across = (((1,), (1,)), ((), ()))
    feat, hidden_size = win_ref.shape
    grad_in = jnp.zeros((feat, hidden_size), F32)
    grad_out = jnp.zeros((8, hidden_size), F32)
    grad_bias = jnp.zeros((8, hidden_size), F32)
    ones = jnp.ones((8, chunk), BF16)
    for x in range(span):
        columns = cols_ref[:, x * chunk : (x + 1) * chunk]
        before = lax.dot_general(win_ref[...], columns, DOWN, preferred_element_type=F32) + bias_ref[...]
        gate = jax.nn.sigmoid(before)
        hidden = (before * gate).astype(BF16)
        up = upstream[:, x * chunk : (x + 1) * chunk].astype(BF16)
        grad_out = grad_out + lax.dot_general(up, hidden, across, preferred_element_type=F32)
        grad_hidden = lax.dot_general(wout_ref[...], up[0:3], DOWN, preferred_element_type=F32)
        grad_before = grad_hidden * (gate * (1.0 + before * (1.0 - gate)))
        high = grad_before.astype(BF16)
        low = (grad_before - high.astype(F32)).astype(BF16)
        grad_bias = grad_bias + lax.dot_general(ones, high, across, preferred_element_type=F32)
        grad_bias = grad_bias + lax.dot_general(ones, low, across, preferred_element_type=F32)
        grad_in = grad_in + lax.dot_general(columns, high, across, preferred_element_type=F32)
    out_ref[0:feat, :] = grad_in
    out_ref[feat : feat + 8, :] = grad_out
    out_ref[feat + 8 : feat + 16, :] = grad_bias


def gather_kernel(counts, total, block_ref, *refs):
    if total:
        out_ref, all_ref, keep_sem, send_sem, recv_sem = refs
    else:
        all_ref, keep_sem, send_sem, recv_sem = refs
    here = tuple(lax.axis_index(name) for name in AXES)

    def peer(axis, shift):
        where = list(here)
        where[axis] = lax.rem(here[axis] + shift, counts[axis])
        return tuple(where)

    barrier = pltpu.get_barrier_semaphore()
    for axis in range(3):
        for shift in range(1, counts[axis]):
            pl.semaphore_signal(barrier, inc=1, device_id=peer(axis, shift), device_id_type=pl.DeviceIdType.MESH)
    keep = pltpu.make_async_copy(block_ref, all_ref.at[here[0], here[2], here[1]], keep_sem)
    keep.start()
    pl.semaphore_wait(barrier, sum(counts) - 3)
    keep.wait()
    slots = []

    def send(back_x, back_z, axis, shift):
        owner_x = lax.rem(here[0] + counts[0] - back_x, counts[0])
        owner_z = lax.rem(here[2] + counts[2] - back_z, counts[2])
        place = all_ref.at[owner_x, owner_z, here[1]]
        slot = len(slots)
        copy = pltpu.make_async_remote_copy(
            src_ref=place,
            dst_ref=place,
            send_sem=send_sem.at[slot],
            recv_sem=recv_sem.at[slot],
            device_id=peer(axis, shift),
            device_id_type=pl.DeviceIdType.MESH,
        )
        slots.append(copy)
        copy.start()
        return copy

    def arrived(back_x, back_z, axis, shift, slot):
        behind_x = back_x + (shift if axis == 0 else 0)
        behind_z = back_z + (shift if axis == 2 else 0)
        place = all_ref.at[
            lax.rem(here[0] + counts[0] - behind_x, counts[0]),
            lax.rem(here[2] + counts[2] - behind_z, counts[2]),
            lax.rem(here[1] + shift, counts[1]) if axis == 1 else here[1],
        ]
        pltpu.make_async_remote_copy(
            src_ref=place,
            dst_ref=place,
            send_sem=send_sem.at[slot],
            recv_sem=recv_sem.at[slot],
            device_id=peer(axis, shift),
            device_id_type=pl.DeviceIdType.MESH,
        ).wait_recv()

    along_z = []
    for shift in range(1, counts[2]):
        along_z.append((shift, len(slots)))
        send(0, 0, 2, shift)
    along_x = []
    along_y = []

    def spread_plane(back_z):
        for shift in range(1, counts[0]):
            along_x.append((shift, back_z, len(slots)))
            send(0, back_z, 0, shift)

    def pass_over(back_x, back_z):
        for shift in range(1, counts[1]):
            along_y.append((back_x, back_z, shift, len(slots)))
            send(back_x, back_z, 1, shift)

    spread_plane(0)
    pass_over(0, 0)
    for shift, slot in along_z:
        arrived(0, 0, 2, shift, slot)
        spread_plane(shift)
        pass_over(0, shift)
    for shift, back_z, slot in along_x:
        arrived(0, back_z, 0, shift, slot)
        pass_over(shift, back_z)
    for back_x, back_z, shift, slot in along_y:
        arrived(back_x, back_z, 1, counts[1] - shift, slot)
    for copy in slots:
        copy.wait_send()
    if total:
        result = jnp.zeros(out_ref.shape, F32)
        for i in range(counts[0]):
            for k in range(counts[2]):
                for j in range(counts[1]):
                    result = result + all_ref[i, k, j]
        out_ref[...] = result


def gather_blocks(block, counts, ident, total=False):
    vmem = pl.BlockSpec(memory_space=pltpu.VMEM)
    steps = counts[2] - 1 + counts[2] * (counts[0] - 1) + counts[0] * counts[2] * (counts[1] - 1)
    every = (counts[0], counts[2], counts[1]) + block.shape
    sems = [pltpu.SemaphoreType.DMA, pltpu.SemaphoreType.DMA((steps,)), pltpu.SemaphoreType.DMA((steps,))]
    held = [pltpu.VMEM(every, F32)] if total else []
    return pl.pallas_call(
        functools.partial(gather_kernel, counts, total),
        out_shape=jax.ShapeDtypeStruct(block.shape if total else every, F32),
        in_specs=[vmem],
        out_specs=vmem,
        scratch_shapes=held + sems,
        compiler_params=pltpu.CompilerParams(
            collective_id=ident, has_side_effects=True, vmem_limit_bytes=VMEM_BYTES
        ),
        name="gather_" + str(ident),
    )(block)


def whole_device(counts, velocity, features, density, target, weight_in, bias_in, weight_out, open_faces):
    shape = density.shape
    span, rows, lanes = shape
    whole = tuple(n * c for n, c in zip(shape, counts))
    feat, hidden_size = weight_in.shape
    cells = span * rows * lanes
    columns = features.reshape(feat, cells)
    bias = bias_in.reshape(hidden_size, 1)
    vmem = pl.BlockSpec(memory_space=pltpu.VMEM)
    smem = pl.BlockSpec(memory_space=pltpu.SMEM)
    params = pltpu.CompilerParams(vmem_limit_bytes=VMEM_BYTES)
    field = jax.ShapeDtypeStruct((3,) + shape, F32)
    message = jax.ShapeDtypeStruct((span + 3, rows, lanes), F32)
    flux, msg = pl.pallas_call(
        functools.partial(forward_kernel, counts),
        out_shape=(field, jax.ShapeDtypeStruct((2 * span + 3, rows, lanes), F32)),
        in_specs=[smem] + [vmem] * 6,
        out_specs=(vmem, vmem),
        scratch_shapes=[pltpu.VMEM((3,) + shape, F32)],
        compiler_params=params,
        name="closure_forward",
    )(open_faces, columns, density, velocity, weight_in, bias, weight_out.T)
    blocks = gather_blocks(msg, counts, 1)
    padded = pltpu.VMEM((whole[0] + 2,) + whole[1:], F32)
    wide = pltpu.VMEM((6, span) + whole[1:], F32)
    folded = pltpu.VMEM((whole[1] + 2, whole[0], whole[2]), F32)
    scratch = [folded, folded, padded, wide] + level_scratch(whole)
    new_velocity, misfit, msg = pl.pallas_call(
        functools.partial(project_kernel, counts),
        out_shape=(field, field, message),
        in_specs=[smem] + [vmem] * 3,
        out_specs=(vmem, vmem, vmem),
        scratch_shapes=scratch,
        compiler_params=params,
        name="project",
    )(open_faces, blocks, flux, target)
    sources = gather_blocks(msg, counts, 2)
    sums = pl.pallas_call(
        functools.partial(adjoint_kernel, counts),
        out_shape=jax.ShapeDtypeStruct((feat + 16, hidden_size), F32),
        in_specs=[smem] + [vmem] * 7,
        out_specs=vmem,
        scratch_shapes=[pltpu.VMEM((8, cells), F32)] + scratch,
        compiler_params=params,
        name="adjoint",
    )(open_faces, blocks, sources, misfit, columns, weight_in, bias, weight_out.T)
    sums = gather_blocks(sums, counts, 3, total=True)
    return new_velocity, sums[:feat], sums[feat + 8], sums[feat : feat + 3].T


def fits(mesh):
    return mesh.size <= 32


def solution(mesh):
    in_specs = (
        P(None, "gx", "gy", "gz"),
        P(None, "gx", "gy", "gz"),
        P("gx", "gy", "gz"),
        P(None, "gx", "gy", "gz"),
        P(),
        P(),
        P(),
        P(),
    )
    out_specs = (P(None, "gx", "gy", "gz"), P(), P(), P())
    counts = tuple(mesh.shape[name] for name in ("gx", "gy", "gz"))
    body = functools.partial(whole_device, counts) if fits(mesh) else per_device
    return jax.shard_map(
        body, mesh=mesh, in_specs=in_specs, out_specs=out_specs, check_vma=False
    )
```
